32 devices in a mesh: cand: 4 (over x, core), prompt: 4 (over z), tensor: 2 (over y).
Axes of the slice: x: 2, y: 2, z: 4, core: 2. Of those that a mesh axis runs over, the one named last changes fastest.
Arguments:
- owner_index: int32 [4], P('prompt'), may hold values from 0 to 3
- suffix_lengths: int32 [4, 4], P('prompt', 'cand'), may hold values from 64 to 256, as said below
- queries: bfloat16 [4, 1024, 8192], P('prompt', 'cand', 'tensor'), may hold values from -15 to 15
- suffix_kv: bfloat16 [2, 4, 1024, 1024], P(None, 'prompt', 'cand', 'tensor'), may hold values from -6 to 6
- prompt_cache: bfloat16 [2, 4, 4, 4096, 1024], P(None, 'prompt', 'cand', None, 'tensor'), may hold values from -6 to 6
- out_weight: bfloat16 [8192, 4096], P('tensor', 'prompt'), may hold values from -0.09375 to 0.09375
Outputs:
- projected: bfloat16 [4, 1024, 4096], P(None, 'cand', ('prompt', 'tensor'))
The draws below stay inside these ranges and needn't reach their ends.
Inputs may be any that keep to these rules, and one draw needn't show every extreme that they name: `suffix_lengths`: the first candidate of every prompt has all 256 suffix tokens live.
All inputs are finite; a program needn't handle non-finite values.
Results may differ from the reference program's by a relative error of at most 0.0057.
Values may be sent and summed in bfloat16 or wider, within the bound.
A program may use at most 128 MiB of HBM per device.

```python
import math
import jax
import jax.numpy as jnp
from jax import lax

HQ = 64
KVH = 8
HD = 128
DOUT = 4096
PLEN = 4096
SUF = 256
CANDS = 4
N_CAND = 4
N_PROMPT = 4


def draw_suffix_lengths(key, part):
    key = jax.random.fold_in(key, 3)
    lengths = jax.random.randint(key, (N_PROMPT, CANDS), SUF // 4, SUF + 1, jnp.int32)
    return lengths.at[:, 0].set(SUF)


def draw_queries(key, part):
    key = jax.random.fold_in(key, 7)
    draw_shape = (N_PROMPT, CANDS * SUF, HQ * HD)
    sampled = jnp.clip(2.5 * jax.random.normal(key, draw_shape, jnp.float32), -15.0, 15.0)
    return sampled.astype(jnp.bfloat16)


def draw_prompt_cache(key, part):
    key = jax.random.fold_in(key, 5)
    draw_shape = (2, N_PROMPT, N_CAND, PLEN, KVH * HD)
    sampled = jnp.clip(jax.random.normal(key, draw_shape, jnp.float32), -6.0, 6.0)
    return sampled.astype(jnp.bfloat16)


def with_ends(result, rng, least, high):
    longest = result.shape.index(max(result.shape))
    spots = []
    for shift in (0, 1):
        where = [jax.random.randint(jax.random.fold_in(rng, axis), (), 0, length) for axis, length in enumerate(result.shape)]
        where[longest] = (where[longest] + shift) % result.shape[longest]
        spots.append(tuple(where))
    return result.at[spots[0]].set(least).at[spots[1]].set(high)


def spiked(result, stream_key, source, target, parts, factor):
    def block_of(dim):
        return (jnp.arange(result.shape[dim]) // (result.shape[dim] // parts)).reshape((-1,) + (1,) * (result.ndim - 1 - dim))

    near = jax.random.permutation(stream_key, parts)[block_of(target)]
    second = (block_of(target) + parts // 2) % parts
    return jnp.where((block_of(source) == near) | (block_of(source) == second), factor * result, result)


def shard_levels(key, shape, split, smallest, high):
    def one(axis_at, blocks):
        steps = jax.random.uniform(jax.random.fold_in(jax.random.fold_in(key, 6), axis_at), (blocks,), jnp.float32, smallest / len(split), high / len(split))
        return jnp.repeat(jnp.exp(steps), shape[axis_at] // blocks).reshape((-1,) + (1,) * (len(shape) - axis_at - 1))

    level = one(*split[0])
    for cut in split[1:]:
        level = level * one(*cut)
    return level


def normal_values(stream_key, extent, spread, most, split=(), kind=jnp.bfloat16):
    factor_of = shard_levels(stream_key, extent, split, -0.22, 0.18) if split else 1.0
    values = jax.random.normal(stream_key, extent, jnp.float32) * spread * factor_of
    return jnp.minimum(jnp.maximum(values, -most), most).astype(kind)


def gaussian_with(key, extent, width, limit, cuts, heavy, kind=jnp.bfloat16):
    drawn = width * jax.random.normal(key, extent, jnp.float32)
    if cuts:
        drawn = drawn * shard_levels(key, extent, cuts, -0.22, 0.18)
    return jnp.clip(spiked(drawn, jax.random.fold_in(key, 3), *heavy), -limit, limit).astype(kind)


def setup_inputs(seed: int = 0) -> dict:
    key_of = jax.random.split(jax.random.key(seed), 7)
    owner_index = with_ends(jax.random.randint(key_of[0], (N_PROMPT,), 0, N_CAND), jax.random.fold_in(key_of[0], 1), 0, N_CAND - 1).astype(jnp.int32)
    suffix_lengths = draw_suffix_lengths(jax.random.fold_in(key_of[6], 71), 0)
    queries = draw_queries(jax.random.fold_in(key_of[6], 71), 0)
    suffix_kv = normal_values(key_of[3], (2, N_PROMPT, CANDS * SUF, KVH * HD), 1.0, 6.0, ((1, 4), (2, 4), (3, 2)))
    prompt_cache = draw_prompt_cache(jax.random.fold_in(key_of[6], 71), 0)
    out_weight = gaussian_with(key_of[5], (HQ * HD, DOUT), (HQ * HD) ** -0.5, 0.09375, ((0, 2), (1, 4)), (0, 1, 4, 2.0))
    return dict(owner_index=owner_index, suffix_lengths=suffix_lengths, queries=queries, suffix_kv=suffix_kv, prompt_cache=prompt_cache, out_weight=out_weight)


def attend(query_rows, key_rows, value_rows, length):
    row_count = query_rows.shape[0]
    key_count = key_rows.shape[0]
    kv_count = key_rows.shape[1] // HD
    group_size = HQ // KVH
    score_scale = 1.0 / math.sqrt(HD)
    query_heads = query_rows.astype(jnp.float32).reshape(row_count, kv_count, group_size, HD)
    query_heads = query_heads.transpose(1, 2, 0, 3).reshape(kv_count, group_size * row_count, HD)
    key_heads = key_rows.astype(jnp.float32).reshape(key_count, kv_count, HD).transpose(1, 0, 2)
    value_heads = value_rows.astype(jnp.float32).reshape(key_count, kv_count, HD).transpose(1, 0, 2)
    scores = jnp.einsum('hqd,hkd->hqk', query_heads, key_heads) * score_scale
    position = jnp.arange(group_size * row_count, dtype=jnp.int32) % row_count
    column = jnp.arange(key_count, dtype=jnp.int32) - (key_count - row_count)
    allowed = (column[None, :] < 0) | (column[None, :] <= position[:, None]) & (column[None, :] < length)
    scores = jnp.where(allowed[None], scores, -1e+30)
    row_max = lax.optimization_barrier(jnp.max(scores, axis=-1, keepdims=True))
    exponent = jnp.exp(scores - row_max)
    weights = (exponent / lax.optimization_barrier(jnp.sum(exponent, axis=-1, keepdims=True))).astype(jnp.bfloat16)
    produced = jnp.einsum('hqk,hkd->hqd', weights.astype(jnp.float32), value_heads).astype(jnp.bfloat16)
    produced = produced.reshape(kv_count, group_size, row_count, HD).transpose(2, 0, 1, 3)
    return produced.reshape(row_count, kv_count * group_size * HD)

def reference(owner_index, suffix_lengths, queries, suffix_kv, prompt_cache, out_weight):
    results = []
    for prompt_id in range(N_PROMPT):
        prompt_slot = lax.dynamic_index_in_dim(prompt_cache[:, prompt_id], owner_index[prompt_id], axis=1, keepdims=False)

        def per_candidate(candidate):
            start_index = (candidate * SUF).astype(jnp.int32)
            query_rows = lax.dynamic_slice_in_dim(queries[prompt_id], start_index, SUF, 0)
            suffix_part = lax.dynamic_slice_in_dim(suffix_kv[:, prompt_id], start_index, SUF, 1)
            key_rows = jnp.concatenate([prompt_slot[0], suffix_part[0]], axis=0)
            value_rows = jnp.concatenate([prompt_slot[1], suffix_part[1]], axis=0)
            return attend(query_rows, key_rows, value_rows, suffix_lengths[prompt_id, candidate])
        attended = lax.map(per_candidate, jnp.arange(CANDS, dtype=jnp.int32))
        attended = attended.reshape(CANDS * SUF, HQ * HD)
        results.append(jnp.dot(attended, out_weight, preferred_element_type=jnp.float32).astype(jnp.bfloat16))
    return jnp.stack(results)
```

```python
import functools
import math

import jax
import jax.numpy as jnp
from jax import lax
from jax.experimental import pallas as pl
from jax.experimental.pallas import tpu as pltpu
from jax.sharding import PartitionSpec as P

HD = 128
HEADS_PER_STEP = 2
KEY_CHUNK = 1024


def attend_kernel(length_ref, flip_ref, q_ref, mine_ref, other_ref, sk_ref, sv_ref, o_ref, k_buf, v_buf, bias_buf):
    plen = mine_ref.shape[0]
    suf = sk_ref.shape[0]

    @pl.when(pl.program_id(0) == 0)
    def _():
        flip = flip_ref[0] != 0

        @pl.when(flip)
        def _():
            k_buf[0:plen, :] = other_ref[...]
            v_buf[0:plen, 0:HD] = mine_ref[...]

        @pl.when(jnp.logical_not(flip))
        def _():
            k_buf[0:plen, :] = mine_ref[...]
            v_buf[0:plen, 0:HD] = other_ref[...]

        k_buf[plen:, :] = sk_ref[...]
        v_buf[plen:, 0:HD] = sv_ref[...]
        v_buf[:, HD:] = jnp.ones((plen + suf, HD), jnp.bfloat16)
        row = lax.broadcasted_iota(jnp.int32, (suf, suf), 0)
        col = lax.broadcasted_iota(jnp.int32, (suf, suf), 1)
        allowed = (col <= row) & (col < length_ref[0])
        bias_buf[...] = jnp.where(allowed, 0.0, -1e30)

    scale = math.log2(math.e) / math.sqrt(HD)
    chunks = [(s, KEY_CHUNK) for s in range(0, plen, KEY_CHUNK)] + [(plen, suf)]
    for head in range(q_ref.shape[1] // HD):
        q = q_ref[:, head * HD : (head + 1) * HD]
        scores = []
        for start, size in chunks:
            s = lax.dot_general(
                q, k_buf[start : start + size, :], (((1,), (1,)), ((), ())), preferred_element_type=jnp.float32
            )
            if start == plen:
                s = s + bias_buf[...]
            scores.append(s)
        top = functools.reduce(jnp.maximum, [jnp.max(s, axis=1, keepdims=True) for s in scores])
        shift = top * scale
        total = None
        for (start, size), s in zip(chunks, scores):
            p = jnp.exp2(s * scale - shift).astype(jnp.bfloat16)
            part = jnp.dot(p, v_buf[start : start + size, :], preferred_element_type=jnp.float32)
            total = part if total is None else total + part
        o_ref[:, head * HD : (head + 1) * HD] = (total[:, 0:HD] / total[:, HD:]).astype(jnp.bfloat16)


def attend_head(head, length, flip, queries, mine, other, suffix_k, suffix_v, group):
    rows = queries.shape[0]
    suf = suffix_k.shape[0]
    plen = mine.shape[0]
    steps = group // HEADS_PER_STEP
    width = HEADS_PER_STEP * HD
    keys = plen + suf
    return pl.pallas_call(
        attend_kernel,
        grid=(steps,),
        out_shape=jax.ShapeDtypeStruct((rows, group * HD), jnp.bfloat16),
        in_specs=[
            pl.BlockSpec(memory_space=pltpu.SMEM),
            pl.BlockSpec(memory_space=pltpu.SMEM),
            pl.BlockSpec((rows, width), lambda i: (0, head * steps + i)),
            pl.BlockSpec((plen, HD), lambda i: (0, 0)),
            pl.BlockSpec((plen, HD), lambda i: (0, 0)),
            pl.BlockSpec((suf, HD), lambda i: (0, head)),
            pl.BlockSpec((suf, HD), lambda i: (0, head)),
        ],
        out_specs=pl.BlockSpec((rows, width), lambda i: (0, i)),
        scratch_shapes=[
            pltpu.VMEM((keys, HD), jnp.bfloat16),
            pltpu.VMEM((keys, 2 * HD), jnp.bfloat16),
            pltpu.VMEM((suf, suf), jnp.float32),
        ],
        compiler_params=pltpu.CompilerParams(vmem_limit_bytes=48 * 1024 * 1024),
        cost_estimate=pl.CostEstimate(
            flops=16 * group * rows * keys * HD, bytes_accessed=4 * keys * HD, transcendentals=group * rows * keys
        ),
    )(length, flip, queries, mine, other, suffix_k, suffix_v)


def flip_perm(count, bit):
    return [(i, i ^ bit) for i in range(count)]


def body(owner_index, suffix_lengths, queries, suffix_kv, prompt_cache, out_weight):
    cand_count = lax.axis_size("cand")
    prompt_count = lax.axis_size("prompt")
    tensor_count = lax.axis_size("tensor")
    owner = owner_index[0]
    me = lax.axis_index("cand")
    side = me % 2
    rows = queries.shape[1]
    kv_count = suffix_kv.shape[3] // HD
    group = queries.shape[2] // (kv_count * HD)

    cache = prompt_cache[:, 0, 0]
    keep = lax.dynamic_index_in_dim(cache, side, 0, keepdims=False)
    give = lax.dynamic_index_in_dim(cache, 1 - side, 0, keepdims=False)

    def same(bit):
        return (owner & bit) == (me & bit)

    pairs = []
    for head in range(kv_count):
        cols = slice(head * HD, (head + 1) * HD)
        got = lax.ppermute(give[:, cols], "cand", flip_perm(cand_count, 1))
        part = jnp.where(same(1), keep[:, cols], got)
        bit = 2
        while bit < cand_count:
            got = lax.ppermute(part, "cand", flip_perm(cand_count, bit))
            part = jnp.where(same(bit), part, got)
            bit *= 2
        pairs.append((part, lax.ppermute(part, "cand", flip_perm(cand_count, 1))))

    length = suffix_lengths.reshape(1)
    flip = side.reshape(1).astype(jnp.int32)
    query_rows = queries[0]
    gathered = []
    for head in range(kv_count):
        mine, other = pairs[head]
        done = attend_head(
            head, length, flip, query_rows, mine, other, suffix_kv[0, 0], suffix_kv[1, 0], group
        )
        gathered.append(lax.all_gather(done, "prompt", axis=0, tiled=True))

    def project(weight):
        total = None
        for head in range(kv_count):
            piece = weight[head * group * HD : (head + 1) * group * HD]
            part = jnp.dot(gathered[head], piece, preferred_element_type=jnp.float32)
            total = part if total is None else total + part
        return total

    col_count = out_weight.shape[1] // tensor_count
    if tensor_count == 2:
        here = lax.axis_index("tensor")
        theirs = lax.dynamic_slice_in_dim(out_weight, (1 - here) * col_count, col_count, 1)
        ours = lax.dynamic_slice_in_dim(out_weight, here * col_count, col_count, 1)
        sent = project(theirs).astype(jnp.bfloat16)
        arrived = lax.ppermute(sent, "tensor", flip_perm(2, 1))
        result = (project(ours) + arrived.astype(jnp.float32)).astype(jnp.bfloat16)
    else:
        total = project(out_weight)
        result = lax.psum_scatter(total, "tensor", scatter_dimension=1, tiled=True).astype(jnp.bfloat16)
    return result.reshape(prompt_count, rows, col_count)


def solution(mesh):
    in_specs = (
        P("prompt"),
        P("prompt", "cand"),
        P("prompt", "cand", "tensor"),
        P(None, "prompt", "cand", "tensor"),
        P(None, "prompt", "cand", None, "tensor"),
        P("tensor", "prompt"),
    )
    out_specs = P(None, "cand", ("prompt", "tensor"))
    return jax.shard_map(body, mesh=mesh, in_specs=in_specs, out_specs=out_specs, check_vma=False)
```

```python
import functools
import math

import jax
import jax.numpy as jnp
from jax import lax
from jax.experimental import pallas as pl
from jax.experimental.pallas import tpu as pltpu
from jax.sharding import PartitionSpec as P

HD = 128
HEADS_PER_STEP = 2
KEY_CHUNK = 1024


def attend_kernel(length_ref, flip_ref, q_ref, mine_ref, other_ref, sk_ref, sv_ref, o_ref, k_buf, v_buf, bias_buf):
    plen = mine_ref.shape[0]
    suf = sk_ref.shape[0]

    @pl.when(pl.program_id(0) == 0)
    def _():
        flip = flip_ref[0] != 0

        @pl.when(flip)
        def _():
            k_buf[0:plen, :] = other_ref[...]
            v_buf[0:plen, 0:HD] = mine_ref[...]

        @pl.when(jnp.logical_not(flip))
        def _():
            k_buf[0:plen, :] = mine_ref[...]
            v_buf[0:plen, 0:HD] = other_ref[...]

        k_buf[plen:, :] = sk_ref[...]
        v_buf[plen:, 0:HD] = sv_ref[...]
        v_buf[:, HD:] = jnp.ones((plen + suf, HD), jnp.bfloat16)
        row = lax.broadcasted_iota(jnp.int32, (suf, suf), 0)
        col = lax.broadcasted_iota(jnp.int32, (suf, suf), 1)
        allowed = (col <= row) & (col < length_ref[0])
        bias_buf[...] = jnp.where(allowed, 0.0, -1e30)

    scale = math.log2(math.e) / math.sqrt(HD)
    chunks = [(s, KEY_CHUNK) for s in range(0, plen, KEY_CHUNK)] + [(plen, suf)]
    for head in range(q_ref.shape[1] // HD):
        q = q_ref[:, head * HD : (head + 1) * HD]
        scores = []
        for start, size in chunks:
            s = lax.dot_general(
                q, k_buf[start : start + size, :], (((1,), (1,)), ((), ())), preferred_element_type=jnp.float32
            )
            if start == plen:
                s = s + bias_buf[...]
            scores.append(s)
        top = functools.reduce(jnp.maximum, [jnp.max(s, axis=1, keepdims=True) for s in scores])
        shift = top * scale
        total = None
        for (start, size), s in zip(chunks, scores):
            p = jnp.exp2(s * scale - shift).astype(jnp.bfloat16)
            part = jnp.dot(p, v_buf[start : start + size, :], preferred_element_type=jnp.float32)
            total = part if total is None else total + part
        o_ref[:, head * HD : (head + 1) * HD] = (total[:, 0:HD] / total[:, HD:]).astype(jnp.bfloat16)


def attend_head(head, length, flip, queries, mine, other, suffix_k, suffix_v, group):
    rows = queries.shape[0]
    suf = suffix_k.shape[0]
    plen = mine.shape[0]
    steps = group // HEADS_PER_STEP
    width = HEADS_PER_STEP * HD
    keys = plen + suf
    return pl.pallas_call(
        attend_kernel,
        grid=(steps,),
        out_shape=jax.ShapeDtypeStruct((rows, group * HD), jnp.bfloat16),
        in_specs=[
            pl.BlockSpec(memory_space=pltpu.SMEM),
            pl.BlockSpec(memory_space=pltpu.SMEM),
            pl.BlockSpec((rows, width), lambda i: (0, head * steps + i)),
            pl.BlockSpec((plen, HD), lambda i: (0, 0)),
            pl.BlockSpec((plen, HD), lambda i: (0, 0)),
            pl.BlockSpec((suf, HD), lambda i: (0, head)),
            pl.BlockSpec((suf, HD), lambda i: (0, head)),
        ],
        out_specs=pl.BlockSpec((rows, width), lambda i: (0, i)),
        scratch_shapes=[
            pltpu.VMEM((keys, HD), jnp.bfloat16),
            pltpu.VMEM((keys, 2 * HD), jnp.bfloat16),
            pltpu.VMEM((suf, suf), jnp.float32),
        ],
        compiler_params=pltpu.CompilerParams(vmem_limit_bytes=48 * 1024 * 1024),
        cost_estimate=pl.CostEstimate(
            flops=16 * group * rows * keys * HD, bytes_accessed=4 * keys * HD, transcendentals=group * rows * keys
        ),
    )(length, flip, queries, mine, other, suffix_k, suffix_v)


def flip_perm(count, bit):
    return [(i, i ^ bit) for i in range(count)]


def fused_kernel(
    owner_ref, length_ref, q_ref, suf_ref, cache_ref, w_ref, out_ref,
    keep, got, xgot, other, k_buf, v_buf, bias_buf, att, w_buf, acc, y_send, y_recv,
    keep_sem, core_send, core_recv, x_send, x_recv, swap_send, swap_recv,
    left_send, right_send, z_recv, y_send_sem, y_recv_sem, w_sem,
):
    heads, plen, _ = keep.shape
    prompts, units, rows, width = att.shape
    suf = suf_ref.shape[1]
    me = lax.axis_index("cand")
    z = lax.axis_index("prompt")
    here = lax.axis_index("tensor")
    side = lax.rem(me, 2)
    core = {"cand": me + 1 - 2 * side}
    across = {"cand": lax.rem(me + 2, 4)}
    beside = {"tensor": 1 - here}
    left = {"prompt": z - 1}
    right = {"prompt": z + 1}
    mesh_id = pl.DeviceIdType.MESH
    has_left = z > 0
    has_right = z < prompts - 1

    barrier = pltpu.get_barrier_semaphore()
    for device in (core, across, beside):
        pl.semaphore_signal(barrier, inc=1, device_id=device, device_id_type=mesh_id)

    @pl.when(has_left)
    def _():
        pl.semaphore_signal(barrier, inc=1, device_id=left, device_id_type=mesh_id)

    @pl.when(has_right)
    def _():
        pl.semaphore_signal(barrier, inc=1, device_id=right, device_id_type=mesh_id)

    pl.semaphore_wait(barrier, 3 + has_left.astype(jnp.int32) + has_right.astype(jnp.int32))

    def remote(src, dst, send, recv, device):
        return pltpu.make_async_remote_copy(
            src_ref=src, dst_ref=dst, send_sem=send, recv_sem=recv, device_id=device, device_id_type=mesh_id
        )

    def keep_copy(h):
        return pltpu.make_async_copy(cache_ref.at[side, :, pl.ds(h * HD, HD)], keep.at[h], keep_sem.at[h])

    def core_copy(h):
        return remote(
            cache_ref.at[1 - side, :, pl.ds(h * HD, HD)], got.at[h], core_send.at[h], core_recv.at[h], core
        )

    def x_copy(h):
        return remote(keep.at[h], xgot.at[h], x_send.at[h], x_recv.at[h], across)

    def swap_copy(h):
        return remote(got.at[h], other.at[h], swap_send.at[h], swap_recv.at[h], core)

    def left_copy(p, u):
        return remote(att.at[p, u], att.at[p, u], left_send.at[p, u], z_recv.at[p, u], left)

    def right_copy(p, u):
        return remote(att.at[p, u], att.at[p, u], right_send.at[p, u], z_recv.at[p, u], right)

    def w_copy():
        return pltpu.make_async_copy(w_ref, w_buf, w_sem)

    owner = owner_ref[0]
    same_core = lax.rem(owner, 2) == side
    same_chip = lax.div(owner, 2) == lax.div(me, 2)

    for h in range(heads):
        core_copy(h).start()
        keep_copy(h).start()
    w_copy().start()

    v_buf[:, HD:] = jnp.ones((plen + suf, HD), jnp.bfloat16)
    row = lax.broadcasted_iota(jnp.int32, (suf, suf), 0)
    col = lax.broadcasted_iota(jnp.int32, (suf, suf), 1)
    bias_buf[...] = jnp.where((col <= row) & (col < length_ref[0]), 0.0, -1e30)

    def first(h, carry):
        keep_copy(h).wait()
        core_copy(h).wait_recv()
        keep[h] = jnp.where(same_core, keep[h], got[h])

        @pl.when(h == 0)
        def _():
            x_copy(h).start()

        return carry

    lax.fori_loop(0, heads, first, 0)

    def prepare(h):
        x_copy(h).wait_recv()

        @pl.when(h + 1 < heads)
        def _():
            x_copy(h + 1).start()

        got[h] = jnp.where(same_chip, keep[h], xgot[h])
        swap_copy(h).start()

    prepare(0)
    acc[...] = jnp.zeros_like(acc)
    w_copy().wait()

    def in_range(u):
        return (u >= 0) & (u < units)

    def project(u):
        def block(p, carry):
            acc[p] += jnp.dot(
                att[p, u], w_buf[pl.ds(pl.multiple_of(u * width, width), width), :],
                preferred_element_type=jnp.float32,
            )
            return carry

        lax.fori_loop(0, prompts, block, 0)

    def pieces(u):
        @pl.when((u < units) & has_left)
        def _():
            left_copy(z, u).start()

        @pl.when((u < units) & has_right)
        def _():
            right_copy(z, u).start()

        for hop in range(1, prompts):
            late = u - hop

            @pl.when(in_range(late) & (z >= hop))
            def _():
                right_copy(z - hop, late).wait_recv()

                @pl.when(has_right)
                def _():
                    right_copy(z - hop, late).start()

            @pl.when(in_range(late) & (z + hop < prompts))
            def _():
                left_copy(z + hop, late).wait_recv()

                @pl.when(has_left)
                def _():
                    left_copy(z + hop, late).start()

        @pl.when(in_range(u - prompts + 1))
        def _():
            project(u - prompts + 1)

    scale = math.log2(math.e) / math.sqrt(HD)
    chunks = [(s, KEY_CHUNK) for s in range(0, plen, KEY_CHUNK)] + [(plen, suf)]
    per_step = HEADS_PER_STEP
    group = units * width // (heads * HD)
    steps = group // per_step
    steps_per_unit = width // (per_step * HD)
    units_per_head = units // heads

    def attend(h, carry):
        swap_copy(h).wait_recv()
        k_buf[0:plen, :] = jnp.where(side == 0, got[h], other[h])
        v_buf[0:plen, 0:HD] = jnp.where(side == 0, other[h], got[h])
        cols = pl.ds(pl.multiple_of(h * HD, HD), HD)
        k_buf[plen:, :] = suf_ref[0, :, cols]
        v_buf[plen:, 0:HD] = suf_ref[1, :, cols]

        def step(i, inner):
            @pl.when((i == steps - 1) & (h + 1 < heads))
            def _():
                prepare(h + 1)

            unit = h * units_per_head + i // steps_per_unit
            for j in range(per_step):
                start_col = (h * group + i * per_step + j) * HD
                q = q_ref[:, pl.ds(pl.multiple_of(start_col, HD), HD)]
                scores = []
                for start, size in chunks:
                    s = lax.dot_general(
                        q, k_buf[start : start + size, :], (((1,), (1,)), ((), ())),
                        preferred_element_type=jnp.float32,
                    )
                    if start == plen:
                        s = s + bias_buf[...]
                    scores.append(s)
                top = functools.reduce(jnp.maximum, [jnp.max(s, axis=1, keepdims=True) for s in scores])
                shift = top * scale
                total = None
                for (start, size), s in zip(chunks, scores):
                    p = jnp.exp2(s * scale - shift).astype(jnp.bfloat16)
                    part = jnp.dot(p, v_buf[start : start + size, :], preferred_element_type=jnp.float32)
                    total = part if total is None else total + part
                place = (i % steps_per_unit) * per_step * HD + j * HD
                att[z, unit, :, pl.ds(pl.multiple_of(place, HD), HD)] = (total[:, 0:HD] / total[:, HD:]).astype(
                    jnp.bfloat16
                )

            @pl.when(i % steps_per_unit == steps_per_unit - 1)
            def _():
                pieces(unit)

            return inner

        lax.fori_loop(0, steps, step, 0)
        return carry

    lax.fori_loop(0, heads, attend, 0)

    def finish(u, carry):
        pieces(u)
        return carry

    lax.fori_loop(units, units + prompts - 1, finish, 0)

    col_count = y_send.shape[2]
    theirs = pl.ds(pl.multiple_of((1 - here) * col_count, col_count), col_count)
    ours = pl.ds(pl.multiple_of(here * col_count, col_count), col_count)

    def y_copy(p):
        return remote(y_send.at[p], y_recv.at[p], y_send_sem.at[p], y_recv_sem.at[p], beside)

    def give(p, carry):
        y_send[p] = acc[p, :, theirs].astype(jnp.bfloat16)
        y_copy(p).start()
        return carry

    def take(p, carry):
        y_copy(p).wait()
        out_ref[p] = (acc[p, :, ours] + y_recv[p].astype(jnp.float32)).astype(jnp.bfloat16)
        return carry

    lax.fori_loop(0, prompts, give, 0)
    lax.fori_loop(0, prompts, take, 0)

    for h in range(heads):
        core_copy(h).wait_send()
        x_copy(h).wait_send()
        swap_copy(h).wait_send()

    def drain(u, carry):
        for p in range(prompts):
            @pl.when(has_left & (z <= p))
            def _():
                left_copy(p, u).wait_send()

            @pl.when(has_right & (z >= p))
            def _():
                right_copy(p, u).wait_send()

        return carry

    lax.fori_loop(0, units, drain, 0)


def fused(owner_index, suffix_lengths, queries, suffix_kv, prompt_cache, out_weight):
    prompts = lax.axis_size("prompt")
    rows, features = queries.shape[1:]
    plen = prompt_cache.shape[3]
    heads = prompt_cache.shape[4] // HD
    suf = suffix_kv.shape[2]
    units = 2 * heads
    width = features // units
    columns = out_weight.shape[1]
    col_count = columns // 2
    keys = plen + suf
    half = pltpu.VMEM((heads, plen, HD), jnp.bfloat16)
    dma = pltpu.SemaphoreType.DMA
    vmem = pl.BlockSpec(memory_space=pltpu.VMEM)
    smem = pl.BlockSpec(memory_space=pltpu.SMEM)
    hbm = pl.BlockSpec(memory_space=pl.ANY)
    return pl.pallas_call(
        fused_kernel,
        out_shape=jax.ShapeDtypeStruct((prompts, rows, col_count), jnp.bfloat16),
        in_specs=[smem, smem, vmem, vmem, hbm, hbm],
        out_specs=vmem,
        scratch_shapes=[
            half, half, half, half,
            pltpu.VMEM((keys, HD), jnp.bfloat16),
            pltpu.VMEM((keys, 2 * HD), jnp.bfloat16),
            pltpu.VMEM((suf, suf), jnp.float32),
            pltpu.VMEM((prompts, units, rows, width), jnp.bfloat16),
            pltpu.VMEM((features, columns), jnp.bfloat16),
            pltpu.VMEM((prompts, rows, columns), jnp.float32),
            pltpu.VMEM((prompts, rows, col_count), jnp.bfloat16),
            pltpu.VMEM((prompts, rows, col_count), jnp.bfloat16),
            dma((heads,)), dma((heads,)), dma((heads,)), dma((heads,)), dma((heads,)), dma((heads,)), dma((heads,)),
            dma((prompts, units)), dma((prompts, units)), dma((prompts, units)),
            dma((prompts,)), dma((prompts,)), dma,
        ],
        compiler_params=pltpu.CompilerParams(
            collective_id=0, has_side_effects=True, vmem_limit_bytes=60 * 1024 * 1024
        ),
        cost_estimate=pl.CostEstimate(
            flops=4 * rows * features * keys + 2 * prompts * rows * features * columns,
            bytes_accessed=4 * plen * heads * HD + 2 * features * columns,
            transcendentals=rows * (features // HD) * keys,
        ),
    )(
        owner_index, suffix_lengths.reshape(1), queries[0], suffix_kv[:, 0], prompt_cache[:, 0, 0], out_weight
    )


def body(owner_index, suffix_lengths, queries, suffix_kv, prompt_cache, out_weight):
    cand_count = lax.axis_size("cand")
    prompt_count = lax.axis_size("prompt")
    tensor_count = lax.axis_size("tensor")
    if (cand_count, prompt_count, tensor_count) == (4, 4, 2):
        return fused(owner_index, suffix_lengths, queries, suffix_kv, prompt_cache, out_weight)
    owner = owner_index[0]
    me = lax.axis_index("cand")
    side = me % 2
    rows = queries.shape[1]
    kv_count = suffix_kv.shape[3] // HD
    group = queries.shape[2] // (kv_count * HD)

    cache = prompt_cache[:, 0, 0]
    keep = lax.dynamic_index_in_dim(cache, side, 0, keepdims=False)
    give = lax.dynamic_index_in_dim(cache, 1 - side, 0, keepdims=False)

    def same(bit):
        return (owner & bit) == (me & bit)

    pairs = []
    for head in range(kv_count):
        cols = slice(head * HD, (head + 1) * HD)
        got = lax.ppermute(give[:, cols], "cand", flip_perm(cand_count, 1))
        part = jnp.where(same(1), keep[:, cols], got)
        bit = 2
        while bit < cand_count:
            got = lax.ppermute(part, "cand", flip_perm(cand_count, bit))
            part = jnp.where(same(bit), part, got)
            bit *= 2
        pairs.append((part, lax.ppermute(part, "cand", flip_perm(cand_count, 1))))

    length = suffix_lengths.reshape(1)
    flip = side.reshape(1).astype(jnp.int32)
    query_rows = queries[0]
    gathered = []
    for head in range(kv_count):
        mine, other = pairs[head]
        done = attend_head(
            head, length, flip, query_rows, mine, other, suffix_kv[0, 0], suffix_kv[1, 0], group
        )
        gathered.append(lax.all_gather(done, "prompt", axis=0, tiled=True))

    def project(weight):
        total = None
        for head in range(kv_count):
            piece = weight[head * group * HD : (head + 1) * group * HD]
            part = jnp.dot(gathered[head], piece, preferred_element_type=jnp.float32)
            total = part if total is None else total + part
        return total

    col_count = out_weight.shape[1] // tensor_count
    if tensor_count == 2:
        here = lax.axis_index("tensor")
        theirs = lax.dynamic_slice_in_dim(out_weight, (1 - here) * col_count, col_count, 1)
        ours = lax.dynamic_slice_in_dim(out_weight, here * col_count, col_count, 1)
        sent = project(theirs).astype(jnp.bfloat16)
        arrived = lax.ppermute(sent, "tensor", flip_perm(2, 1))
        result = (project(ours) + arrived.astype(jnp.float32)).astype(jnp.bfloat16)
    else:
        total = project(out_weight)
        result = lax.psum_scatter(total, "tensor", scatter_dimension=1, tiled=True).astype(jnp.bfloat16)
    return result.reshape(prompt_count, rows, col_count)


def solution(mesh):
    in_specs = (
        P("prompt"),
        P("prompt", "cand"),
        P("prompt", "cand", "tensor"),
        P(None, "prompt", "cand", "tensor"),
        P(None, "prompt", "cand", None, "tensor"),
        P("tensor", "prompt"),
    )
    out_specs = P(None, "cand", ("prompt", "tensor"))
    return jax.shard_map(body, mesh=mesh, in_specs=in_specs, out_specs=out_specs, check_vma=False)
```

```python
import functools
import math

import jax
import jax.numpy as jnp
from jax import lax
from jax.experimental import pallas as pl
from jax.experimental.pallas import tpu as pltpu
from jax.sharding import PartitionSpec as P

HD = 128
HEADS_PER_STEP = 2
KEY_CHUNK = 1024


def attend_kernel(length_ref, flip_ref, q_ref, mine_ref, other_ref, sk_ref, sv_ref, o_ref, k_buf, v_buf, bias_buf):
    plen = mine_ref.shape[0]
    suf = sk_ref.shape[0]

    @pl.when(pl.program_id(0) == 0)
    def _():
        flip = flip_ref[0] != 0

        @pl.when(flip)
        def _():
            k_buf[0:plen, :] = other_ref[...]
            v_buf[0:plen, 0:HD] = mine_ref[...]

        @pl.when(jnp.logical_not(flip))
        def _():
            k_buf[0:plen, :] = mine_ref[...]
            v_buf[0:plen, 0:HD] = other_ref[...]

        k_buf[plen:, :] = sk_ref[...]
        v_buf[plen:, 0:HD] = sv_ref[...]
        v_buf[:, HD:] = jnp.ones((plen + suf, HD), jnp.bfloat16)
        row = lax.broadcasted_iota(jnp.int32, (suf, suf), 0)
        col = lax.broadcasted_iota(jnp.int32, (suf, suf), 1)
        allowed = (col <= row) & (col < length_ref[0])
        bias_buf[...] = jnp.where(allowed, 0.0, -1e30)

    scale = math.log2(math.e) / math.sqrt(HD)
    chunks = [(s, KEY_CHUNK) for s in range(0, plen, KEY_CHUNK)] + [(plen, suf)]
    for head in range(q_ref.shape[1] // HD):
        q = q_ref[:, head * HD : (head + 1) * HD]
        scores = []
        for start, size in chunks:
            s = lax.dot_general(
                q, k_buf[start : start + size, :], (((1,), (1,)), ((), ())), preferred_element_type=jnp.float32
            )
            if start == plen:
                s = s + bias_buf[...]
            scores.append(s)
        top = functools.reduce(jnp.maximum, [jnp.max(s, axis=1, keepdims=True) for s in scores])
        shift = top * scale
        total = None
        for (start, size), s in zip(chunks, scores):
            p = jnp.exp2(s * scale - shift).astype(jnp.bfloat16)
            part = jnp.dot(p, v_buf[start : start + size, :], preferred_element_type=jnp.float32)
            total = part if total is None else total + part
        o_ref[:, head * HD : (head + 1) * HD] = (total[:, 0:HD] / total[:, HD:]).astype(jnp.bfloat16)


def attend_head(head, length, flip, queries, mine, other, suffix_k, suffix_v, group):
    rows = queries.shape[0]
    suf = suffix_k.shape[0]
    plen = mine.shape[0]
    steps = group // HEADS_PER_STEP
    width = HEADS_PER_STEP * HD
    keys = plen + suf
    return pl.pallas_call(
        attend_kernel,
        grid=(steps,),
        out_shape=jax.ShapeDtypeStruct((rows, group * HD), jnp.bfloat16),
        in_specs=[
            pl.BlockSpec(memory_space=pltpu.SMEM),
            pl.BlockSpec(memory_space=pltpu.SMEM),
            pl.BlockSpec((rows, width), lambda i: (0, head * steps + i)),
            pl.BlockSpec((plen, HD), lambda i: (0, 0)),
            pl.BlockSpec((plen, HD), lambda i: (0, 0)),
            pl.BlockSpec((suf, HD), lambda i: (0, head)),
            pl.BlockSpec((suf, HD), lambda i: (0, head)),
        ],
        out_specs=pl.BlockSpec((rows, width), lambda i: (0, i)),
        scratch_shapes=[
            pltpu.VMEM((keys, HD), jnp.bfloat16),
            pltpu.VMEM((keys, 2 * HD), jnp.bfloat16),
            pltpu.VMEM((suf, suf), jnp.float32),
        ],
        compiler_params=pltpu.CompilerParams(vmem_limit_bytes=48 * 1024 * 1024),
        cost_estimate=pl.CostEstimate(
            flops=16 * group * rows * keys * HD, bytes_accessed=4 * keys * HD, transcendentals=group * rows * keys
        ),
    )(length, flip, queries, mine, other, suffix_k, suffix_v)


def flip_perm(count, bit):
    return [(i, i ^ bit) for i in range(count)]


def fused_kernel(
    owner_ref, length_ref, q_ref, suf_ref, cache_ref, w_ref, out_ref, near_ref,
    keep, got, xgot, other, k_buf, v_buf, bias_buf, att, w_buf, acc, y_send, y_recv,
    near_buf, near_acc, near_send, near_recv, near_done, near_in,
    keep_sem, core_send, core_recv, x_send, x_recv, swap_send, swap_recv,
    left_send, right_send, z_recv, y_send_sem, y_recv_sem, w_sem,
    near_z_send, near_z_recv, near_core_send, near_core_recv, near_sem,
    near_y_send, near_y_recv, near_out_send, near_out_recv,
):
    heads, plen, _ = keep.shape
    prompts, units, rows, width = att.shape
    suf = suf_ref.shape[1]
    me = lax.axis_index("cand")
    z = lax.axis_index("prompt")
    here = lax.axis_index("tensor")
    side = lax.rem(me, 2)
    core = {"cand": me + 1 - 2 * side}
    across = {"cand": lax.rem(me + 2, 4)}
    beside = {"tensor": 1 - here}
    left = {"prompt": z - 1}
    right = {"prompt": z + 1}
    mesh_id = pl.DeviceIdType.MESH
    has_left = z > 0
    has_right = z < prompts - 1

    barrier = pltpu.get_barrier_semaphore()
    for device in (core, across, beside):
        pl.semaphore_signal(barrier, inc=1, device_id=device, device_id_type=mesh_id)

    @pl.when(has_left)
    def _():
        pl.semaphore_signal(barrier, inc=1, device_id=left, device_id_type=mesh_id)

    @pl.when(has_right)
    def _():
        pl.semaphore_signal(barrier, inc=1, device_id=right, device_id_type=mesh_id)

    pl.semaphore_wait(barrier, 3 + has_left.astype(jnp.int32) + has_right.astype(jnp.int32))

    def remote(src, dst, send, recv, device):
        return pltpu.make_async_remote_copy(
            src_ref=src, dst_ref=dst, send_sem=send, recv_sem=recv, device_id=device, device_id_type=mesh_id
        )

    def keep_copy(h):
        return pltpu.make_async_copy(cache_ref.at[side, :, pl.ds(h * HD, HD)], keep.at[h], keep_sem.at[h])

    def core_copy(h):
        return remote(
            cache_ref.at[1 - side, :, pl.ds(h * HD, HD)], got.at[h], core_send.at[h], core_recv.at[h], core
        )

    def x_copy(h):
        return remote(keep.at[h], xgot.at[h], x_send.at[h], x_recv.at[h], across)

    def swap_copy(h):
        return remote(got.at[h], other.at[h], swap_send.at[h], swap_recv.at[h], core)

    def left_copy(p, u):
        return remote(att.at[p, u], att.at[p, u], left_send.at[p, u], z_recv.at[p, u], left)

    def right_copy(p, u):
        return remote(att.at[p, u], att.at[p, u], right_send.at[p, u], z_recv.at[p, u], right)

    def w_copy():
        return pltpu.make_async_copy(w_ref, w_buf, w_sem)

    inner = (z == 1) | (z == 2)
    outer = (z == 0) | (z == prompts - 1)
    inward = {"prompt": 1 + z // 3}
    outward = {"prompt": (z - 1) * 3}

    def unit_rows(u):
        return pl.ds(pl.multiple_of(u * width, width), width)

    def near_z_copy(j):
        part = unit_rows(2 * j + side)
        return remote(w_ref.at[part], near_ref.at[part], near_z_send.at[j], near_z_recv.at[j], inward)

    def near_core_copy(j):
        part = unit_rows(2 * j + side)
        return remote(near_ref.at[part], near_ref.at[part], near_core_send.at[j], near_core_recv.at[j], core)

    def near_load(j):
        part = pl.ds(pl.multiple_of(2 * j * width, 2 * width), 2 * width)
        return pltpu.make_async_copy(near_ref.at[part], near_buf, near_sem)

    def near_y_copy():
        return remote(near_send, near_recv, near_y_send, near_y_recv, beside)

    def near_out_copy():
        return remote(near_done, near_in, near_out_send, near_out_recv, outward)

    def y_copy(p):
        return remote(y_send.at[p], y_recv.at[p], y_send_sem.at[p], y_recv_sem.at[p], beside)

    col_count = y_send.shape[2]
    theirs = pl.ds(pl.multiple_of((1 - here) * col_count, col_count), col_count)
    ours = pl.ds(pl.multiple_of(here * col_count, col_count), col_count)

    owner = owner_ref[0]
    same_core = lax.rem(owner, 2) == side
    same_chip = lax.div(owner, 2) == lax.div(me, 2)

    for h in range(heads):
        core_copy(h).start()
        keep_copy(h).start()
    w_copy().start()

    @pl.when(outer)
    def _():
        for j in range(units // 2):
            near_z_copy(j).start()

    v_buf[:, HD:] = jnp.ones((plen + suf, HD), jnp.bfloat16)
    row = lax.broadcasted_iota(jnp.int32, (suf, suf), 0)
    col = lax.broadcasted_iota(jnp.int32, (suf, suf), 1)
    bias_buf[...] = jnp.where((col <= row) & (col < length_ref[0]), 0.0, -1e30)

    def first(h, carry):
        keep_copy(h).wait()
        core_copy(h).wait_recv()
        keep[h] = jnp.where(same_core, keep[h], got[h])

        @pl.when(h == 0)
        def _():
            x_copy(h).start()

        return carry

    lax.fori_loop(0, heads, first, 0)

    def prepare(h):
        x_copy(h).wait_recv()

        @pl.when(h + 1 < heads)
        def _():
            x_copy(h + 1).start()

        got[h] = jnp.where(same_chip, keep[h], xgot[h])
        swap_copy(h).start()

    prepare(0)
    acc[...] = jnp.zeros_like(acc)
    near_acc[...] = jnp.zeros_like(near_acc)
    w_copy().wait()

    def in_range(u):
        return (u >= 0) & (u < units)

    def project(p, u):
        acc[p] += jnp.dot(att[p, u], w_buf[unit_rows(u), :], preferred_element_type=jnp.float32)

        @pl.when(u == units - 1)
        def _():
            y_send[p] = acc[p, :, theirs].astype(jnp.bfloat16)
            y_copy(p).start()

    def lend(u):
        @pl.when(inner & (u == units // 2))
        def _():
            for j in range(units // 2):
                near_z_copy(j).wait_recv()
                near_core_copy(j).start()

        @pl.when(inner & (u > units // 2) & (u < units))
        def _():
            low = u - units // 2 - 1

            def pair(j, carry):
                near_core_copy(j).wait_recv()
                near_load(j).start()
                near_load(j).wait()
                for k in range(2):
                    near_acc[...] += jnp.dot(
                        att[z, 2 * j + k], near_buf[k * width : (k + 1) * width, :],
                        preferred_element_type=jnp.float32,
                    )
                return carry

            lax.fori_loop(low, jnp.where(u == units - 1, units // 2, low + 1), pair, 0)

        @pl.when(inner & (u == units - 1))
        def _():
            near_send[...] = near_acc[:, theirs].astype(jnp.bfloat16)
            near_y_copy().start()

        @pl.when(inner & (u == units))
        def _():
            near_y_copy().wait()
            near_done[...] = (near_acc[:, ours] + near_recv[...].astype(jnp.float32)).astype(jnp.bfloat16)
            near_out_copy().start()

    def pieces(u):
        @pl.when((u < units) & has_left & (z != 1))
        def _():
            left_copy(z, u).start()

        @pl.when((u < units) & has_right & (z != prompts - 2))
        def _():
            right_copy(z, u).start()

        lend(u)

        @pl.when(u < units)
        def _():
            project(z, u)

        for hop in range(1, prompts):
            late = u - hop
            from_left = (z >= hop) if hop > 1 else inner
            from_right = (z + hop < prompts) if hop > 1 else inner

            @pl.when(in_range(late) & from_left)
            def _():
                right_copy(z - hop, late).wait_recv()

                @pl.when(has_right)
                def _():
                    right_copy(z - hop, late).start()

            @pl.when(in_range(late) & from_right)
            def _():
                left_copy(z + hop, late).wait_recv()

                @pl.when(has_left)
                def _():
                    left_copy(z + hop, late).start()

            @pl.when(in_range(late) & from_left)
            def _():
                project(z - hop, late)

            @pl.when(in_range(late) & from_right)
            def _():
                project(z + hop, late)

    scale = math.log2(math.e) / math.sqrt(HD)
    chunks = [(s, KEY_CHUNK) for s in range(0, plen, KEY_CHUNK)] + [(plen, suf)]
    per_step = HEADS_PER_STEP
    group = units * width // (heads * HD)
    steps = group // per_step
    steps_per_unit = width // (per_step * HD)
    units_per_head = units // heads

    def attend(h, carry):
        swap_copy(h).wait_recv()
        k_buf[0:plen, :] = jnp.where(side == 0, got[h], other[h])
        v_buf[0:plen, 0:HD] = jnp.where(side == 0, other[h], got[h])
        cols = pl.ds(pl.multiple_of(h * HD, HD), HD)
        k_buf[plen:, :] = suf_ref[0, :, cols]
        v_buf[plen:, 0:HD] = suf_ref[1, :, cols]

        def step(i, inner):
            @pl.when((i == steps - 1) & (h + 1 < heads))
            def _():
                prepare(h + 1)

            unit = h * units_per_head + i // steps_per_unit
            start_col = (h * group + i * per_step) * HD
            q = jnp.concatenate(
                [q_ref[:, pl.ds(pl.multiple_of(start_col + j * HD, HD), HD)] for j in range(per_step)], axis=0
            )
            scores = []
            for start, size in chunks:
                s = lax.dot_general(
                    q, k_buf[start : start + size, :], (((1,), (1,)), ((), ())),
                    preferred_element_type=jnp.float32,
                )
                if start == plen:
                    s = s + jnp.concatenate([bias_buf[...]] * per_step, axis=0)
                scores.append(s)
            top = functools.reduce(jnp.maximum, [jnp.max(s, axis=1, keepdims=True) for s in scores])
            shift = top * scale
            total = None
            for (start, size), s in zip(chunks, scores):
                p = jnp.exp2(s * scale - shift).astype(jnp.bfloat16)
                part = jnp.dot(p, v_buf[start : start + size, :], preferred_element_type=jnp.float32)
                total = part if total is None else total + part
            place = (i % steps_per_unit) * per_step * HD
            done = (total[:, 0:HD] / total[:, HD:]).astype(jnp.bfloat16)
            for j in range(per_step):
                att[z, unit, :, pl.ds(pl.multiple_of(place + j * HD, HD), HD)] = done[j * rows : (j + 1) * rows]

            @pl.when(i % steps_per_unit == steps_per_unit - 1)
            def _():
                pieces(unit)

            return inner

        lax.fori_loop(0, steps, step, 0)
        return carry

    lax.fori_loop(0, heads, attend, 0)

    def finish(u, carry):
        pieces(u)
        return carry

    lax.fori_loop(units, units + prompts - 1, finish, 0)

    for p in range(prompts):
        borrowed = outer & (p == 1 + z // 3)

        @pl.when(jnp.logical_not(borrowed))
        def _():
            y_copy(p).wait()
            out_ref[p] = (acc[p, :, ours] + y_recv[p].astype(jnp.float32)).astype(jnp.bfloat16)

        @pl.when(borrowed)
        def _():
            near_out_copy().wait_recv()
            out_ref[p] = near_in[...]

    for h in range(heads):
        core_copy(h).wait_send()
        x_copy(h).wait_send()
        swap_copy(h).wait_send()

    @pl.when(outer)
    def _():
        for j in range(units // 2):
            near_z_copy(j).wait_send()

    @pl.when(inner)
    def _():
        for j in range(units // 2):
            near_core_copy(j).wait_send()
        near_out_copy().wait_send()

    def drain(u, carry):
        for p in range(prompts):
            @pl.when(has_left & ((z < p) | (z == p) & (z != 1)))
            def _():
                left_copy(p, u).wait_send()

            @pl.when(has_right & ((z > p) | (z == p) & (z != prompts - 2)))
            def _():
                right_copy(p, u).wait_send()

        return carry

    lax.fori_loop(0, units, drain, 0)


def fused(owner_index, suffix_lengths, queries, suffix_kv, prompt_cache, out_weight):
    prompts = lax.axis_size("prompt")
    rows, features = queries.shape[1:]
    plen = prompt_cache.shape[3]
    heads = prompt_cache.shape[4] // HD
    suf = suffix_kv.shape[2]
    units = 2 * heads
    width = features // units
    columns = out_weight.shape[1]
    col_count = columns // 2
    keys = plen + suf
    half = pltpu.VMEM((heads, plen, HD), jnp.bfloat16)
    block = pltpu.VMEM((rows, col_count), jnp.bfloat16)
    dma = pltpu.SemaphoreType.DMA
    vmem = pl.BlockSpec(memory_space=pltpu.VMEM)
    smem = pl.BlockSpec(memory_space=pltpu.SMEM)
    hbm = pl.BlockSpec(memory_space=pl.ANY)
    return pl.pallas_call(
        fused_kernel,
        out_shape=[
            jax.ShapeDtypeStruct((prompts, rows, col_count), jnp.bfloat16),
            jax.ShapeDtypeStruct((features, columns), jnp.bfloat16),
        ],
        in_specs=[smem, smem, vmem, vmem, hbm, hbm],
        out_specs=[vmem, hbm],
        scratch_shapes=[
            half, half, half, half,
            pltpu.VMEM((keys, HD), jnp.bfloat16),
            pltpu.VMEM((keys, 2 * HD), jnp.bfloat16),
            pltpu.VMEM((suf, suf), jnp.float32),
            pltpu.VMEM((prompts, units, rows, width), jnp.bfloat16),
            pltpu.VMEM((features, columns), jnp.bfloat16),
            pltpu.VMEM((prompts, rows, columns), jnp.float32),
            pltpu.VMEM((prompts, rows, col_count), jnp.bfloat16),
            pltpu.VMEM((prompts, rows, col_count), jnp.bfloat16),
            pltpu.VMEM((2 * width, columns), jnp.bfloat16),
            pltpu.VMEM((rows, columns), jnp.float32),
            block, block, block, block,
            dma((heads,)), dma((heads,)), dma((heads,)), dma((heads,)), dma((heads,)), dma((heads,)), dma((heads,)),
            dma((prompts, units)), dma((prompts, units)), dma((prompts, units)),
            dma((prompts,)), dma((prompts,)), dma,
            dma((units // 2,)), dma((units // 2,)), dma((units // 2,)), dma((units // 2,)), dma, dma, dma, dma, dma,
        ],
        compiler_params=pltpu.CompilerParams(
            collective_id=0, has_side_effects=True, vmem_limit_bytes=62 * 1024 * 1024
        ),
        cost_estimate=pl.CostEstimate(
            flops=4 * rows * features * keys + 2 * prompts * rows * features * columns,
            bytes_accessed=4 * plen * heads * HD + 2 * features * columns,
            transcendentals=rows * (features // HD) * keys,
        ),
    )(
        owner_index, suffix_lengths.reshape(1), queries[0], suffix_kv[:, 0], prompt_cache[:, 0, 0], out_weight
    )[0]


def body(owner_index, suffix_lengths, queries, suffix_kv, prompt_cache, out_weight):
    cand_count = lax.axis_size("cand")
    prompt_count = lax.axis_size("prompt")
    tensor_count = lax.axis_size("tensor")
    if (cand_count, prompt_count, tensor_count) == (4, 4, 2):
        return fused(owner_index, suffix_lengths, queries, suffix_kv, prompt_cache, out_weight)
    owner = owner_index[0]
    me = lax.axis_index("cand")
    side = me % 2
    rows = queries.shape[1]
    kv_count = suffix_kv.shape[3] // HD
    group = queries.shape[2] // (kv_count * HD)

    cache = prompt_cache[:, 0, 0]
    keep = lax.dynamic_index_in_dim(cache, side, 0, keepdims=False)
    give = lax.dynamic_index_in_dim(cache, 1 - side, 0, keepdims=False)

    def same(bit):
        return (owner & bit) == (me & bit)

    pairs = []
    for head in range(kv_count):
        cols = slice(head * HD, (head + 1) * HD)
        got = lax.ppermute(give[:, cols], "cand", flip_perm(cand_count, 1))
        part = jnp.where(same(1), keep[:, cols], got)
        bit = 2
        while bit < cand_count:
            got = lax.ppermute(part, "cand", flip_perm(cand_count, bit))
            part = jnp.where(same(bit), part, got)
            bit *= 2
        pairs.append((part, lax.ppermute(part, "cand", flip_perm(cand_count, 1))))

    length = suffix_lengths.reshape(1)
    flip = side.reshape(1).astype(jnp.int32)
    query_rows = queries[0]
    gathered = []
    for head in range(kv_count):
        mine, other = pairs[head]
        done = attend_head(
            head, length, flip, query_rows, mine, other, suffix_kv[0, 0], suffix_kv[1, 0], group
        )
        gathered.append(lax.all_gather(done, "prompt", axis=0, tiled=True))

    def project(weight):
        total = None
        for head in range(kv_count):
            piece = weight[head * group * HD : (head + 1) * group * HD]
            part = jnp.dot(gathered[head], piece, preferred_element_type=jnp.float32)
            total = part if total is None else total + part
        return total

    col_count = out_weight.shape[1] // tensor_count
    if tensor_count == 2:
        here = lax.axis_index("tensor")
        theirs = lax.dynamic_slice_in_dim(out_weight, (1 - here) * col_count, col_count, 1)
        ours = lax.dynamic_slice_in_dim(out_weight, here * col_count, col_count, 1)
        sent = project(theirs).astype(jnp.bfloat16)
        arrived = lax.ppermute(sent, "tensor", flip_perm(2, 1))
        result = (project(ours) + arrived.astype(jnp.float32)).astype(jnp.bfloat16)
    else:
        total = project(out_weight)
        result = lax.psum_scatter(total, "tensor", scatter_dimension=1, tiled=True).astype(jnp.bfloat16)
    return result.reshape(prompt_count, rows, col_count)


def solution(mesh):
    in_specs = (
        P("prompt"),
        P("prompt", "cand"),
        P("prompt", "cand", "tensor"),
        P(None, "prompt", "cand", "tensor"),
        P(None, "prompt", "cand", None, "tensor"),
        P("tensor", "prompt"),
    )
    out_specs = P(None, "cand", ("prompt", "tensor"))
    return jax.shard_map(body, mesh=mesh, in_specs=in_specs, out_specs=out_specs, check_vma=False)
```

```python
import functools
import math

import jax
import jax.numpy as jnp
from jax import lax
from jax.experimental import pallas as pl
from jax.experimental.pallas import tpu as pltpu
from jax.sharding import PartitionSpec as P

HD = 128
HEADS_PER_STEP = 2
KEY_CHUNK = 1024


def attend_kernel(length_ref, flip_ref, q_ref, mine_ref, other_ref, sk_ref, sv_ref, o_ref, k_buf, v_buf, bias_buf):
    plen = mine_ref.shape[0]
    suf = sk_ref.shape[0]

    @pl.when(pl.program_id(0) == 0)
    def _():
        flip = flip_ref[0] != 0

        @pl.when(flip)
        def _():
            k_buf[0:plen, :] = other_ref[...]
            v_buf[0:plen, 0:HD] = mine_ref[...]

        @pl.when(jnp.logical_not(flip))
        def _():
            k_buf[0:plen, :] = mine_ref[...]
            v_buf[0:plen, 0:HD] = other_ref[...]

        k_buf[plen:, :] = sk_ref[...]
        v_buf[plen:, 0:HD] = sv_ref[...]
        v_buf[:, HD:] = jnp.ones((plen + suf, HD), jnp.bfloat16)
        row = lax.broadcasted_iota(jnp.int32, (suf, suf), 0)
        col = lax.broadcasted_iota(jnp.int32, (suf, suf), 1)
        allowed = (col <= row) & (col < length_ref[0])
        bias_buf[...] = jnp.where(allowed, 0.0, -1e30)

    scale = math.log2(math.e) / math.sqrt(HD)
    chunks = [(s, KEY_CHUNK) for s in range(0, plen, KEY_CHUNK)] + [(plen, suf)]
    for head in range(q_ref.shape[1] // HD):
        q = q_ref[:, head * HD : (head + 1) * HD]
        scores = []
        for start, size in chunks:
            s = lax.dot_general(
                q, k_buf[start : start + size, :], (((1,), (1,)), ((), ())), preferred_element_type=jnp.float32
            )
            if start == plen:
                s = s + bias_buf[...]
            scores.append(s)
        top = functools.reduce(jnp.maximum, [jnp.max(s, axis=1, keepdims=True) for s in scores])
        shift = top * scale
        total = None
        for (start, size), s in zip(chunks, scores):
            p = jnp.exp2(s * scale - shift).astype(jnp.bfloat16)
            part = jnp.dot(p, v_buf[start : start + size, :], preferred_element_type=jnp.float32)
            total = part if total is None else total + part
        o_ref[:, head * HD : (head + 1) * HD] = (total[:, 0:HD] / total[:, HD:]).astype(jnp.bfloat16)


def attend_head(head, length, flip, queries, mine, other, suffix_k, suffix_v, group):
    rows = queries.shape[0]
    suf = suffix_k.shape[0]
    plen = mine.shape[0]
    steps = group // HEADS_PER_STEP
    width = HEADS_PER_STEP * HD
    keys = plen + suf
    return pl.pallas_call(
        attend_kernel,
        grid=(steps,),
        out_shape=jax.ShapeDtypeStruct((rows, group * HD), jnp.bfloat16),
        in_specs=[
            pl.BlockSpec(memory_space=pltpu.SMEM),
            pl.BlockSpec(memory_space=pltpu.SMEM),
            pl.BlockSpec((rows, width), lambda i: (0, head * steps + i)),
            pl.BlockSpec((plen, HD), lambda i: (0, 0)),
            pl.BlockSpec((plen, HD), lambda i: (0, 0)),
            pl.BlockSpec((suf, HD), lambda i: (0, head)),
            pl.BlockSpec((suf, HD), lambda i: (0, head)),
        ],
        out_specs=pl.BlockSpec((rows, width), lambda i: (0, i)),
        scratch_shapes=[
            pltpu.VMEM((keys, HD), jnp.bfloat16),
            pltpu.VMEM((keys, 2 * HD), jnp.bfloat16),
            pltpu.VMEM((suf, suf), jnp.float32),
        ],
        compiler_params=pltpu.CompilerParams(vmem_limit_bytes=48 * 1024 * 1024),
        cost_estimate=pl.CostEstimate(
            flops=16 * group * rows * keys * HD, bytes_accessed=4 * keys * HD, transcendentals=group * rows * keys
        ),
    )(length, flip, queries, mine, other, suffix_k, suffix_v)


def flip_perm(count, bit):
    return [(i, i ^ bit) for i in range(count)]


def fused_kernel(
    owner_ref, length_ref, q_ref, suf_ref, cache_ref, w_ref, out_ref, near_ref,
    keep, got, xgot, other, k_buf, v_buf, bias_buf, att, w_buf, acc, y_send, y_recv,
    near_buf, near_acc, near_send, near_recv, near_done, near_in,
    keep_sem, core_send, core_recv, x_send, x_recv, swap_send, swap_recv,
    left_send, right_send, z_recv, y_send_sem, y_recv_sem, w_sem,
    near_z_send, near_z_recv, near_core_send, near_core_recv, near_sem,
    near_y_send, near_y_recv, near_out_send, near_out_recv,
):
    heads, plen, _ = keep.shape
    prompts, units, rows, width = att.shape
    suf = suf_ref.shape[1]
    me = lax.axis_index("cand")
    z = lax.axis_index("prompt")
    here = lax.axis_index("tensor")
    side = lax.rem(me, 2)
    core = {"cand": me + 1 - 2 * side}
    across = {"cand": lax.rem(me + 2, 4)}
    beside = {"tensor": 1 - here}
    left = {"prompt": z - 1}
    right = {"prompt": z + 1}
    mesh_id = pl.DeviceIdType.MESH
    has_left = z > 0
    has_right = z < prompts - 1

    barrier = pltpu.get_barrier_semaphore()
    for device in (core, across, beside):
        pl.semaphore_signal(barrier, inc=1, device_id=device, device_id_type=mesh_id)

    @pl.when(has_left)
    def _():
        pl.semaphore_signal(barrier, inc=1, device_id=left, device_id_type=mesh_id)

    @pl.when(has_right)
    def _():
        pl.semaphore_signal(barrier, inc=1, device_id=right, device_id_type=mesh_id)

    pl.semaphore_wait(barrier, 3 + has_left.astype(jnp.int32) + has_right.astype(jnp.int32))

    def remote(src, dst, send, recv, device):
        return pltpu.make_async_remote_copy(
            src_ref=src, dst_ref=dst, send_sem=send, recv_sem=recv, device_id=device, device_id_type=mesh_id
        )

    def keep_copy(h):
        return pltpu.make_async_copy(cache_ref.at[side, :, pl.ds(h * HD, HD)], keep.at[h], keep_sem.at[h])

    def core_copy(h):
        return remote(
            cache_ref.at[1 - side, :, pl.ds(h * HD, HD)], got.at[h], core_send.at[h], core_recv.at[h], core
        )

    def x_copy(h):
        return remote(keep.at[h], xgot.at[h], x_send.at[h], x_recv.at[h], across)

    def swap_copy(h):
        return remote(got.at[h], other.at[h], swap_send.at[h], swap_recv.at[h], core)

    def left_copy(p, u):
        return remote(att.at[p, u], att.at[p, u], left_send.at[p, u], z_recv.at[p, u], left)

    def right_copy(p, u):
        return remote(att.at[p, u], att.at[p, u], right_send.at[p, u], z_recv.at[p, u], right)

    def w_copy():
        return pltpu.make_async_copy(w_ref, w_buf, w_sem)

    inner = (z == 1) | (z == 2)
    outer = (z == 0) | (z == prompts - 1)
    inward = {"prompt": 1 + z // 3}
    outward = {"prompt": (z - 1) * 3}

    def unit_rows(u):
        return pl.ds(pl.multiple_of(u * width, width), width)

    def near_z_copy(j):
        part = unit_rows(2 * j + side)
        return remote(w_ref.at[part], near_ref.at[part], near_z_send.at[j], near_z_recv.at[j], inward)

    def near_core_copy(j):
        part = unit_rows(2 * j + side)
        return remote(near_ref.at[part], near_ref.at[part], near_core_send.at[j], near_core_recv.at[j], core)

    def near_load(j):
        part = pl.ds(pl.multiple_of(2 * j * width, 2 * width), 2 * width)
        return pltpu.make_async_copy(near_ref.at[part], near_buf, near_sem)

    def near_y_copy():
        return remote(near_send, near_recv, near_y_send, near_y_recv, beside)

    def near_out_copy():
        return remote(near_done, near_in, near_out_send, near_out_recv, outward)

    def y_copy(p):
        return remote(y_send.at[p], y_recv.at[p], y_send_sem.at[p], y_recv_sem.at[p], beside)

    col_count = y_send.shape[2]
    theirs = pl.ds(pl.multiple_of((1 - here) * col_count, col_count), col_count)
    ours = pl.ds(pl.multiple_of(here * col_count, col_count), col_count)

    owner = owner_ref[0]
    same_core = lax.rem(owner, 2) == side
    same_chip = lax.div(owner, 2) == lax.div(me, 2)

    for h in range(heads):
        core_copy(h).start()
        keep_copy(h).start()
    w_copy().start()

    @pl.when(outer)
    def _():
        for j in range(units // 2):
            near_z_copy(j).start()

    v_buf[:, HD:] = jnp.ones((plen + suf, HD), jnp.bfloat16)
    row = lax.broadcasted_iota(jnp.int32, (suf, suf), 0)
    col = lax.broadcasted_iota(jnp.int32, (suf, suf), 1)
    bias_buf[...] = jnp.where((col <= row) & (col < length_ref[0]), 0.0, -1e30)

    def first(h, carry):
        keep_copy(h).wait()
        core_copy(h).wait_recv()
        keep[h] = jnp.where(same_core, keep[h], got[h])

        @pl.when(h == 0)
        def _():
            x_copy(h).start()

        return carry

    lax.fori_loop(0, heads, first, 0)

    def prepare(h):
        x_copy(h).wait_recv()

        @pl.when(h + 1 < heads)
        def _():
            x_copy(h + 1).start()

        got[h] = jnp.where(same_chip, keep[h], xgot[h])
        swap_copy(h).start()

    prepare(0)
    acc[...] = jnp.zeros_like(acc)
    near_acc[...] = jnp.zeros_like(near_acc)
    w_copy().wait()

    def in_range(u):
        return (u >= 0) & (u < units)

    def project(p, u):
        acc[p] += jnp.dot(att[p, u], w_buf[unit_rows(u), :], preferred_element_type=jnp.float32)

        @pl.when(u == units - 1)
        def _():
            y_send[p] = acc[p, :, theirs].astype(jnp.bfloat16)
            y_copy(p).start()

    def lend(u):
        @pl.when(inner & (u == units // 2))
        def _():
            for j in range(units // 2):
                near_z_copy(j).wait_recv()
                near_core_copy(j).start()

        @pl.when(inner & (u > units // 2) & (u < units))
        def _():
            low = u - units // 2 - 1

            def pair(j, carry):
                near_core_copy(j).wait_recv()
                near_load(j).start()
                near_load(j).wait()
                for k in range(2):
                    near_acc[...] += jnp.dot(
                        att[z, 2 * j + k], near_buf[k * width : (k + 1) * width, :],
                        preferred_element_type=jnp.float32,
                    )
                return carry

            lax.fori_loop(low, jnp.where(u == units - 1, units // 2, low + 1), pair, 0)

        @pl.when(inner & (u == units - 1))
        def _():
            near_send[...] = near_acc[:, theirs].astype(jnp.bfloat16)
            near_y_copy().start()

        @pl.when(inner & (u == units))
        def _():
            near_y_copy().wait()
            near_done[...] = (near_acc[:, ours] + near_recv[...].astype(jnp.float32)).astype(jnp.bfloat16)
            near_out_copy().start()

    def pieces(u):
        @pl.when((u < units) & has_left & (z != 1))
        def _():
            left_copy(z, u).start()

        @pl.when((u < units) & has_right & (z != prompts - 2))
        def _():
            right_copy(z, u).start()

        lend(u)

        @pl.when(u < units)
        def _():
            project(z, u)

        for hop in range(1, prompts):
            late = u - hop
            from_left = (z >= hop) if hop > 1 else inner
            from_right = (z + hop < prompts) if hop > 1 else inner

            @pl.when(in_range(late) & from_left)
            def _():
                right_copy(z - hop, late).wait_recv()

                @pl.when(has_right)
                def _():
                    right_copy(z - hop, late).start()

            @pl.when(in_range(late) & from_right)
            def _():
                left_copy(z + hop, late).wait_recv()

                @pl.when(has_left)
                def _():
                    left_copy(z + hop, late).start()

            @pl.when(in_range(late) & from_left)
            def _():
                project(z - hop, late)

            @pl.when(in_range(late) & from_right)
            def _():
                project(z + hop, late)

    scale = math.log2(math.e) / math.sqrt(HD)
    chunks = [(s, KEY_CHUNK) for s in range(0, plen, KEY_CHUNK)] + [(plen, suf)]
    per_step = HEADS_PER_STEP
    group = units * width // (heads * HD)
    steps = group // per_step
    steps_per_unit = width // (per_step * HD)
    units_per_head = units // heads

    def attend(h, carry):
        swap_copy(h).wait_recv()
        k_buf[0:plen, :] = jnp.where(side == 0, got[h], other[h])
        v_buf[0:plen, 0:HD] = jnp.where(side == 0, other[h], got[h])
        cols = pl.ds(pl.multiple_of(h * HD, HD), HD)
        k_buf[plen:, :] = suf_ref[0, :, cols]
        v_buf[plen:, 0:HD] = suf_ref[1, :, cols]

        def step(i, inner):
            @pl.when((i == steps - 1) & (h + 1 < heads))
            def _():
                prepare(h + 1)

            unit = h * units_per_head + i // steps_per_unit
            for j in range(per_step):
                start_col = (h * group + i * per_step + j) * HD
                q = q_ref[:, pl.ds(pl.multiple_of(start_col, HD), HD)]
                scores = []
                for start, size in chunks:
                    s = lax.dot_general(
                        q, k_buf[start : start + size, :], (((1,), (1,)), ((), ())),
                        preferred_element_type=jnp.float32,
                    )
                    if start == plen:
                        s = s + bias_buf[...]
                    scores.append(s)
                top = functools.reduce(jnp.maximum, [jnp.max(s, axis=1, keepdims=True) for s in scores])
                shift = top * scale
                total = None
                for (start, size), s in zip(chunks, scores):
                    p = jnp.exp2(s * scale - shift).astype(jnp.bfloat16)
                    part = jnp.dot(p, v_buf[start : start + size, :], preferred_element_type=jnp.float32)
                    total = part if total is None else total + part
                place = (i % steps_per_unit) * per_step * HD + j * HD
                att[z, unit, :, pl.ds(pl.multiple_of(place, HD), HD)] = (total[:, 0:HD] / total[:, HD:]).astype(
                    jnp.bfloat16
                )

            @pl.when(i % steps_per_unit == steps_per_unit - 1)
            def _():
                pieces(unit)

            return inner

        lax.fori_loop(0, steps, step, 0)
        return carry

    lax.fori_loop(0, heads, attend, 0)

    def finish(u, carry):
        pieces(u)
        return carry

    lax.fori_loop(units, units + prompts - 1, finish, 0)

    for p in range(prompts):
        borrowed = outer & (p == 1 + z // 3)

        @pl.when(jnp.logical_not(borrowed))
        def _():
            y_copy(p).wait()
            out_ref[p] = (acc[p, :, ours] + y_recv[p].astype(jnp.float32)).astype(jnp.bfloat16)

        @pl.when(borrowed)
        def _():
            near_out_copy().wait_recv()
            out_ref[p] = near_in[...]

    for h in range(heads):
        core_copy(h).wait_send()
        x_copy(h).wait_send()
        swap_copy(h).wait_send()

    @pl.when(outer)
    def _():
        for j in range(units // 2):
            near_z_copy(j).wait_send()

    @pl.when(inner)
    def _():
        for j in range(units // 2):
            near_core_copy(j).wait_send()
        near_out_copy().wait_send()

    def drain(u, carry):
        for p in range(prompts):
            @pl.when(has_left & ((z < p) | (z == p) & (z != 1)))
            def _():
                left_copy(p, u).wait_send()

            @pl.when(has_right & ((z > p) | (z == p) & (z != prompts - 2)))
            def _():
                right_copy(p, u).wait_send()

        return carry

    lax.fori_loop(0, units, drain, 0)


def fused(owner_index, suffix_lengths, queries, suffix_kv, prompt_cache, out_weight):
    prompts = lax.axis_size("prompt")
    rows, features = queries.shape[1:]
    plen = prompt_cache.shape[3]
    heads = prompt_cache.shape[4] // HD
    suf = suffix_kv.shape[2]
    units = 2 * heads
    width = features // units
    columns = out_weight.shape[1]
    col_count = columns // 2
    keys = plen + suf
    half = pltpu.VMEM((heads, plen, HD), jnp.bfloat16)
    block = pltpu.VMEM((rows, col_count), jnp.bfloat16)
    dma = pltpu.SemaphoreType.DMA
    vmem = pl.BlockSpec(memory_space=pltpu.VMEM)
    smem = pl.BlockSpec(memory_space=pltpu.SMEM)
    hbm = pl.BlockSpec(memory_space=pl.ANY)
    return pl.pallas_call(
        fused_kernel,
        out_shape=[
            jax.ShapeDtypeStruct((prompts, rows, col_count), jnp.bfloat16),
            jax.ShapeDtypeStruct((features, columns), jnp.bfloat16),
        ],
        in_specs=[smem, smem, vmem, vmem, hbm, hbm],
        out_specs=[vmem, hbm],
        scratch_shapes=[
            half, half, half, half,
            pltpu.VMEM((keys, HD), jnp.bfloat16),
            pltpu.VMEM((keys, 2 * HD), jnp.bfloat16),
            pltpu.VMEM((suf, suf), jnp.float32),
            pltpu.VMEM((prompts, units, rows, width), jnp.bfloat16),
            pltpu.VMEM((features, columns), jnp.bfloat16),
            pltpu.VMEM((prompts, rows, columns), jnp.float32),
            pltpu.VMEM((prompts, rows, col_count), jnp.bfloat16),
            pltpu.VMEM((prompts, rows, col_count), jnp.bfloat16),
            pltpu.VMEM((2 * width, columns), jnp.bfloat16),
            pltpu.VMEM((rows, columns), jnp.float32),
            block, block, block, block,
            dma((heads,)), dma((heads,)), dma((heads,)), dma((heads,)), dma((heads,)), dma((heads,)), dma((heads,)),
            dma((prompts, units)), dma((prompts, units)), dma((prompts, units)),
            dma((prompts,)), dma((prompts,)), dma,
            dma((units // 2,)), dma((units // 2,)), dma((units // 2,)), dma((units // 2,)), dma, dma, dma, dma, dma,
        ],
        compiler_params=pltpu.CompilerParams(
            collective_id=0, has_side_effects=True, vmem_limit_bytes=62 * 1024 * 1024
        ),
        cost_estimate=pl.CostEstimate(
            flops=4 * rows * features * keys + 2 * prompts * rows * features * columns,
            bytes_accessed=4 * plen * heads * HD + 2 * features * columns,
            transcendentals=rows * (features // HD) * keys,
        ),
    )(
        owner_index, suffix_lengths.reshape(1), queries[0], suffix_kv[:, 0], prompt_cache[:, 0, 0], out_weight
    )[0]


def body(owner_index, suffix_lengths, queries, suffix_kv, prompt_cache, out_weight):
    cand_count = lax.axis_size("cand")
    prompt_count = lax.axis_size("prompt")
    tensor_count = lax.axis_size("tensor")
    if (cand_count, prompt_count, tensor_count) == (4, 4, 2):
        return fused(owner_index, suffix_lengths, queries, suffix_kv, prompt_cache, out_weight)
    owner = owner_index[0]
    me = lax.axis_index("cand")
    side = me % 2
    rows = queries.shape[1]
    kv_count = suffix_kv.shape[3] // HD
    group = queries.shape[2] // (kv_count * HD)

    cache = prompt_cache[:, 0, 0]
    keep = lax.dynamic_index_in_dim(cache, side, 0, keepdims=False)
    give = lax.dynamic_index_in_dim(cache, 1 - side, 0, keepdims=False)

    def same(bit):
        return (owner & bit) == (me & bit)

    pairs = []
    for head in range(kv_count):
        cols = slice(head * HD, (head + 1) * HD)
        got = lax.ppermute(give[:, cols], "cand", flip_perm(cand_count, 1))
        part = jnp.where(same(1), keep[:, cols], got)
        bit = 2
        while bit < cand_count:
            got = lax.ppermute(part, "cand", flip_perm(cand_count, bit))
            part = jnp.where(same(bit), part, got)
            bit *= 2
        pairs.append((part, lax.ppermute(part, "cand", flip_perm(cand_count, 1))))

    length = suffix_lengths.reshape(1)
    flip = side.reshape(1).astype(jnp.int32)
    query_rows = queries[0]
    gathered = []
    for head in range(kv_count):
        mine, other = pairs[head]
        done = attend_head(
            head, length, flip, query_rows, mine, other, suffix_kv[0, 0], suffix_kv[1, 0], group
        )
        gathered.append(lax.all_gather(done, "prompt", axis=0, tiled=True))

    def project(weight):
        total = None
        for head in range(kv_count):
            piece = weight[head * group * HD : (head + 1) * group * HD]
            part = jnp.dot(gathered[head], piece, preferred_element_type=jnp.float32)
            total = part if total is None else total + part
        return total

    col_count = out_weight.shape[1] // tensor_count
    if tensor_count == 2:
        here = lax.axis_index("tensor")
        theirs = lax.dynamic_slice_in_dim(out_weight, (1 - here) * col_count, col_count, 1)
        ours = lax.dynamic_slice_in_dim(out_weight, here * col_count, col_count, 1)
        sent = project(theirs).astype(jnp.bfloat16)
        arrived = lax.ppermute(sent, "tensor", flip_perm(2, 1))
        result = (project(ours) + arrived.astype(jnp.float32)).astype(jnp.bfloat16)
    else:
        total = project(out_weight)
        result = lax.psum_scatter(total, "tensor", scatter_dimension=1, tiled=True).astype(jnp.bfloat16)
    return result.reshape(prompt_count, rows, col_count)


def solution(mesh):
    in_specs = (
        P("prompt"),
        P("prompt", "cand"),
        P("prompt", "cand", "tensor"),
        P(None, "prompt", "cand", "tensor"),
        P(None, "prompt", "cand", None, "tensor"),
        P("tensor", "prompt"),
    )
    out_specs = P(None, "cand", ("prompt", "tensor"))
    return jax.shard_map(body, mesh=mesh, in_specs=in_specs, out_specs=out_specs, check_vma=False)
```

```python
import functools
import math

import jax
import jax.numpy as jnp
from jax import lax
from jax.experimental import pallas as pl
from jax.experimental.pallas import tpu as pltpu
from jax.sharding import PartitionSpec as P

HD = 128
HEADS_PER_STEP = 2
KEY_CHUNK = 1024


def attend_kernel(length_ref, flip_ref, q_ref, mine_ref, other_ref, sk_ref, sv_ref, o_ref, k_buf, v_buf, bias_buf):
    plen = mine_ref.shape[0]
    suf = sk_ref.shape[0]

    @pl.when(pl.program_id(0) == 0)
    def _():
        flip = flip_ref[0] != 0

        @pl.when(flip)
        def _():
            k_buf[0:plen, :] = other_ref[...]
            v_buf[0:plen, 0:HD] = mine_ref[...]

        @pl.when(jnp.logical_not(flip))
        def _():
            k_buf[0:plen, :] = mine_ref[...]
            v_buf[0:plen, 0:HD] = other_ref[...]

        k_buf[plen:, :] = sk_ref[...]
        v_buf[plen:, 0:HD] = sv_ref[...]
        v_buf[:, HD:] = jnp.ones((plen + suf, HD), jnp.bfloat16)
        row = lax.broadcasted_iota(jnp.int32, (suf, suf), 0)
        col = lax.broadcasted_iota(jnp.int32, (suf, suf), 1)
        allowed = (col <= row) & (col < length_ref[0])
        bias_buf[...] = jnp.where(allowed, 0.0, -1e30)

    scale = math.log2(math.e) / math.sqrt(HD)
    chunks = [(s, KEY_CHUNK) for s in range(0, plen, KEY_CHUNK)] + [(plen, suf)]
    for head in range(q_ref.shape[1] // HD):
        q = q_ref[:, head * HD : (head + 1) * HD]
        scores = []
        for start, size in chunks:
            s = lax.dot_general(
                q, k_buf[start : start + size, :], (((1,), (1,)), ((), ())), preferred_element_type=jnp.float32
            )
            if start == plen:
                s = s + bias_buf[...]
            scores.append(s)
        top = functools.reduce(jnp.maximum, [jnp.max(s, axis=1, keepdims=True) for s in scores])
        shift = top * scale
        total = None
        for (start, size), s in zip(chunks, scores):
            p = jnp.exp2(s * scale - shift).astype(jnp.bfloat16)
            part = jnp.dot(p, v_buf[start : start + size, :], preferred_element_type=jnp.float32)
            total = part if total is None else total + part
        o_ref[:, head * HD : (head + 1) * HD] = (total[:, 0:HD] / total[:, HD:]).astype(jnp.bfloat16)


def attend_head(head, length, flip, queries, mine, other, suffix_k, suffix_v, group):
    rows = queries.shape[0]
    suf = suffix_k.shape[0]
    plen = mine.shape[0]
    steps = group // HEADS_PER_STEP
    width = HEADS_PER_STEP * HD
    keys = plen + suf
    return pl.pallas_call(
        attend_kernel,
        grid=(steps,),
        out_shape=jax.ShapeDtypeStruct((rows, group * HD), jnp.bfloat16),
        in_specs=[
            pl.BlockSpec(memory_space=pltpu.SMEM),
            pl.BlockSpec(memory_space=pltpu.SMEM),
            pl.BlockSpec((rows, width), lambda i: (0, head * steps + i)),
            pl.BlockSpec((plen, HD), lambda i: (0, 0)),
            pl.BlockSpec((plen, HD), lambda i: (0, 0)),
            pl.BlockSpec((suf, HD), lambda i: (0, head)),
            pl.BlockSpec((suf, HD), lambda i: (0, head)),
        ],
        out_specs=pl.BlockSpec((rows, width), lambda i: (0, i)),
        scratch_shapes=[
            pltpu.VMEM((keys, HD), jnp.bfloat16),
            pltpu.VMEM((keys, 2 * HD), jnp.bfloat16),
            pltpu.VMEM((suf, suf), jnp.float32),
        ],
        compiler_params=pltpu.CompilerParams(vmem_limit_bytes=48 * 1024 * 1024),
        cost_estimate=pl.CostEstimate(
            flops=16 * group * rows * keys * HD, bytes_accessed=4 * keys * HD, transcendentals=group * rows * keys
        ),
    )(length, flip, queries, mine, other, suffix_k, suffix_v)


def flip_perm(count, bit):
    return [(i, i ^ bit) for i in range(count)]


def fused_kernel(
    owner_ref, length_ref, q_ref, suf_ref, cache_ref, w_ref, out_ref, near_ref,
    keep, got, xgot, other, k_buf, v_buf, bias_buf, att, w_buf, acc, y_send, y_recv,
    near_buf, near_acc, near_send, near_recv, near_done, near_in, scores,
    keep_sem, core_send, core_recv, x_send, x_recv, swap_send, swap_recv,
    left_send, right_send, z_recv, y_send_sem, y_recv_sem, w_sem,
    near_z_send, near_z_recv, near_core_send, near_core_recv, near_sem,
    near_y_send, near_y_recv, near_out_send, near_out_recv, q_sem,
):
    heads, plen, _ = keep.shape
    prompts, units, rows, width = att.shape
    suf = suf_ref.shape[1]
    me = lax.axis_index("cand")
    z = lax.axis_index("prompt")
    here = lax.axis_index("tensor")
    side = lax.rem(me, 2)
    core = {"cand": me + 1 - 2 * side}
    across = {"cand": lax.rem(me + 2, 4)}
    beside = {"tensor": 1 - here}
    left = {"prompt": z - 1}
    right = {"prompt": z + 1}
    mesh_id = pl.DeviceIdType.MESH
    has_left = z > 0
    has_right = z < prompts - 1

    barrier = pltpu.get_barrier_semaphore()
    for device in (core, across, beside):
        pl.semaphore_signal(barrier, inc=1, device_id=device, device_id_type=mesh_id)

    @pl.when(has_left)
    def _():
        pl.semaphore_signal(barrier, inc=1, device_id=left, device_id_type=mesh_id)

    @pl.when(has_right)
    def _():
        pl.semaphore_signal(barrier, inc=1, device_id=right, device_id_type=mesh_id)

    pl.semaphore_wait(barrier, 3 + has_left.astype(jnp.int32) + has_right.astype(jnp.int32))

    def remote(src, dst, send, recv, device):
        return pltpu.make_async_remote_copy(
            src_ref=src, dst_ref=dst, send_sem=send, recv_sem=recv, device_id=device, device_id_type=mesh_id
        )

    def keep_copy(h):
        return pltpu.make_async_copy(cache_ref.at[side, :, pl.ds(h * HD, HD)], keep.at[h], keep_sem.at[h])

    def core_copy(h):
        return remote(
            cache_ref.at[1 - side, :, pl.ds(h * HD, HD)], got.at[h], core_send.at[h], core_recv.at[h], core
        )

    def x_copy(h):
        return remote(keep.at[h], xgot.at[h], x_send.at[h], x_recv.at[h], across)

    def swap_copy(h):
        return remote(got.at[h], other.at[h], swap_send.at[h], swap_recv.at[h], core)

    def left_copy(p, u):
        return remote(att.at[p, u], att.at[p, u], left_send.at[p, u], z_recv.at[p, u], left)

    def right_copy(p, u):
        return remote(att.at[p, u], att.at[p, u], right_send.at[p, u], z_recv.at[p, u], right)

    def q_copy(u):
        return pltpu.make_async_copy(q_ref.at[:, pl.ds(u * width, width)], att.at[z, u], q_sem.at[u])

    def w_copy():
        return pltpu.make_async_copy(w_ref, w_buf, w_sem)

    inner = (z == 1) | (z == 2)
    outer = (z == 0) | (z == prompts - 1)
    inward = {"prompt": 1 + z // 3}
    outward = {"prompt": (z - 1) * 3}

    def unit_rows(u):
        return pl.ds(pl.multiple_of(u * width, width), width)

    def near_z_copy(j):
        part = unit_rows(2 * j + side)
        return remote(w_ref.at[part], near_ref.at[part], near_z_send.at[j], near_z_recv.at[j], inward)

    def near_core_copy(j):
        part = unit_rows(2 * j + side)
        return remote(near_ref.at[part], near_ref.at[part], near_core_send.at[j], near_core_recv.at[j], core)

    def near_load(j):
        return pltpu.make_async_copy(near_ref.at[unit_rows(j)], near_buf, near_sem)

    def near_y_copy():
        return remote(near_send, near_recv, near_y_send, near_y_recv, beside)

    def near_out_copy():
        return remote(near_done, near_in, near_out_send, near_out_recv, outward)

    def y_copy(p):
        return remote(y_send.at[p], y_recv.at[p], y_send_sem.at[p], y_recv_sem.at[p], beside)

    col_count = y_send.shape[2]
    theirs = pl.ds(pl.multiple_of((1 - here) * col_count, col_count), col_count)
    ours = pl.ds(pl.multiple_of(here * col_count, col_count), col_count)

    owner = owner_ref[0]
    same_core = lax.rem(owner, 2) == side
    same_chip = lax.div(owner, 2) == lax.div(me, 2)

    for h in range(heads):
        core_copy(h).start()
        keep_copy(h).start()
    for u in range(units):
        q_copy(u).start()
    w_copy().start()

    @pl.when(outer)
    def _():
        for j in range(units // 4):
            near_z_copy(j).start()

    v_buf[:, HD:] = jnp.ones((plen + suf, HD), jnp.bfloat16)
    row = lax.broadcasted_iota(jnp.int32, bias_buf.shape, 0)
    col = lax.broadcasted_iota(jnp.int32, bias_buf.shape, 1) - (bias_buf.shape[1] - suf)
    bias_buf[...] = jnp.where((col < 0) | (col <= row) & (col < length_ref[0]), 0.0, -1e30)

    def first(h, carry):
        keep_copy(h).wait()
        core_copy(h).wait_recv()
        keep[h] = jnp.where(same_core, keep[h], got[h])

        @pl.when(h == 0)
        def _():
            x_copy(h).start()

        return carry

    lax.fori_loop(0, heads, first, 0)

    def prepare(h):
        x_copy(h).wait_recv()

        @pl.when(h + 1 < heads)
        def _():
            x_copy(h + 1).start()

        got[h] = jnp.where(same_chip, keep[h], xgot[h])
        swap_copy(h).start()

    prepare(0)
    acc[...] = jnp.zeros_like(acc)
    near_acc[...] = jnp.zeros_like(near_acc)
    w_copy().wait()
    for u in range(units):
        q_copy(u).wait()

    def in_range(u):
        return (u >= 0) & (u < units)

    def project(p, u):
        acc[p] += jnp.dot(att[p, u], w_buf[unit_rows(u), :], preferred_element_type=jnp.float32)

        @pl.when(u == units - 1)
        def _():
            y_send[p] = acc[p, :, theirs].astype(jnp.bfloat16)
            y_copy(p).start()

    def lend(u):
        for j in range(units // 4, units // 2):
            @pl.when(outer & (u == 2 * j - units // 2 + 1))
            def _():
                near_z_copy(j).start()

        @pl.when(inner & (u == units - 2))
        def _():
            for j in range(units // 2):
                near_z_copy(j).wait_recv()
                near_core_copy(j).start()

        @pl.when(inner & ((u == units - 1) | (u == units)))
        def _():
            low = (u - units + 1) * (units // 4)

            def pair(j, carry):
                near_core_copy(j).wait_recv()
                for k in range(2):
                    near_load(2 * j + k).start()
                    near_load(2 * j + k).wait()
                    near_acc[...] += jnp.dot(att[z, 2 * j + k], near_buf[...], preferred_element_type=jnp.float32)
                return carry

            lax.fori_loop(low, low + units // 4, pair, 0)

        @pl.when(inner & (u == units))
        def _():
            near_send[...] = near_acc[:, theirs].astype(jnp.bfloat16)
            near_y_copy().start()

        @pl.when(inner & (u == units + 1))
        def _():
            near_y_copy().wait()
            near_done[...] = (near_acc[:, ours] + near_recv[...].astype(jnp.float32)).astype(jnp.bfloat16)
            near_out_copy().start()

    def pieces(u):
        @pl.when((u < units) & has_left & (z != 1))
        def _():
            left_copy(z, u).start()

        @pl.when((u < units) & has_right & (z != prompts - 2))
        def _():
            right_copy(z, u).start()

        lend(u)

        @pl.when(u < units)
        def _():
            project(z, u)

        for hop in range(1, prompts):
            late = u - hop - 1
            from_left = (z >= hop) if hop > 1 else inner
            from_right = (z + hop < prompts) if hop > 1 else inner

            @pl.when(in_range(late) & from_left)
            def _():
                right_copy(z - hop, late).wait_recv()

                @pl.when(has_right)
                def _():
                    right_copy(z - hop, late).start()

            @pl.when(in_range(late) & from_right)
            def _():
                left_copy(z + hop, late).wait_recv()

                @pl.when(has_left)
                def _():
                    left_copy(z + hop, late).start()

            @pl.when(in_range(late) & from_left)
            def _():
                project(z - hop, late)

            @pl.when(in_range(late) & from_right)
            def _():
                project(z + hop, late)

    scale = math.log2(math.e) / math.sqrt(HD)
    keys = plen + suf
    starts = list(range(0, plen, KEY_CHUNK))
    chunks = list(zip(starts, starts[1:] + [keys]))
    group = units * width // (heads * HD)
    per_unit = width // HD

    def attend(h, carry):
        swap_copy(h).wait_recv()
        k_buf[0:plen, :] = jnp.where(side == 0, got[h], other[h])
        v_buf[0:plen, 0:HD] = jnp.where(side == 0, other[h], got[h])
        cols = pl.ds(pl.multiple_of(h * HD, HD), HD)
        k_buf[plen:, :] = suf_ref[0, :, cols]
        v_buf[plen:, 0:HD] = suf_ref[1, :, cols]

        def query(i):
            place = (i % per_unit) * HD
            return att[z, (h * group + i) // per_unit, :, pl.ds(pl.multiple_of(place, HD), HD)]

        def score(q, slot, chunk, top):
            start, end = chunk
            s = lax.dot_general(
                q, k_buf[start:end, :], (((1,), (1,)), ((), ())), preferred_element_type=jnp.float32
            )
            if end == keys:
                s = s + bias_buf[...]
            scores[slot, :, start:end] = s
            high = jnp.max(s, axis=1, keepdims=True)
            return high if top is None else jnp.maximum(top, high)

        def weigh(slot, chunk, shift, total):
            start, end = chunk
            p = jnp.exp2(scores[slot, :, start:end] * scale - shift).astype(jnp.bfloat16)
            part = jnp.dot(p, v_buf[start:end, :], preferred_element_type=jnp.float32)
            return part if total is None else total + part

        def store(i, total):
            unit = (h * group + i) // per_unit
            place = (i % per_unit) * HD
            att[z, unit, :, pl.ds(pl.multiple_of(place, HD), HD)] = (total[:, 0:HD] / total[:, HD:]).astype(
                jnp.bfloat16
            )

            @pl.when(i % per_unit == per_unit - 1)
            def _():
                pieces(unit)

        first_query = query(0)
        top = None
        for chunk in chunks:
            top = score(first_query, 0, chunk, top)

        def step(i, top):
            @pl.when((i == group - 3) & (h + 1 < heads))
            def _():
                prepare(h + 1)

            shift = top * scale
            slot = lax.rem(i, 2)
            q = query(i + 1)
            later = None
            total = None
            for chunk in chunks:
                later = score(q, 1 - slot, chunk, later)
                total = weigh(slot, chunk, shift, total)
            store(i, total)
            return later

        top = lax.fori_loop(0, group - 1, step, top)
        shift = top * scale
        total = None
        for chunk in chunks:
            total = weigh((group - 1) % 2, chunk, shift, total)
        store(jnp.int32(group - 1), total)
        return carry

    lax.fori_loop(0, heads, attend, 0)

    def finish(u, carry):
        pieces(u)
        return carry

    lax.fori_loop(units, units + prompts, finish, 0)

    for p in range(prompts):
        borrowed = outer & (p == 1 + z // 3)

        @pl.when(jnp.logical_not(borrowed))
        def _():
            y_copy(p).wait()
            out_ref[p] = (acc[p, :, ours] + y_recv[p].astype(jnp.float32)).astype(jnp.bfloat16)

        @pl.when(borrowed)
        def _():
            near_out_copy().wait_recv()
            out_ref[p] = near_in[...]

    for h in range(heads):
        core_copy(h).wait_send()
        x_copy(h).wait_send()
        swap_copy(h).wait_send()

    @pl.when(outer)
    def _():
        for j in range(units // 2):
            near_z_copy(j).wait_send()

    @pl.when(inner)
    def _():
        for j in range(units // 2):
            near_core_copy(j).wait_send()
        near_out_copy().wait_send()

    def drain(u, carry):
        for p in range(prompts):
            @pl.when(has_left & ((z < p) | (z == p) & (z != 1)))
            def _():
                left_copy(p, u).wait_send()

            @pl.when(has_right & ((z > p) | (z == p) & (z != prompts - 2)))
            def _():
                right_copy(p, u).wait_send()

        return carry

    lax.fori_loop(0, units, drain, 0)


def fused(owner_index, suffix_lengths, queries, suffix_kv, prompt_cache, out_weight):
    prompts = lax.axis_size("prompt")
    rows, features = queries.shape[1:]
    plen = prompt_cache.shape[3]
    heads = prompt_cache.shape[4] // HD
    suf = suffix_kv.shape[2]
    units = 2 * heads
    width = features // units
    columns = out_weight.shape[1]
    col_count = columns // 2
    keys = plen + suf
    half = pltpu.VMEM((heads, plen, HD), jnp.bfloat16)
    block = pltpu.VMEM((rows, col_count), jnp.bfloat16)
    dma = pltpu.SemaphoreType.DMA
    vmem = pl.BlockSpec(memory_space=pltpu.VMEM)
    smem = pl.BlockSpec(memory_space=pltpu.SMEM)
    hbm = pl.BlockSpec(memory_space=pl.ANY)
    return pl.pallas_call(
        fused_kernel,
        out_shape=[
            jax.ShapeDtypeStruct((prompts, rows, col_count), jnp.bfloat16),
            jax.ShapeDtypeStruct((features, columns), jnp.bfloat16),
        ],
        in_specs=[smem, smem, hbm, vmem, hbm, hbm],
        out_specs=[vmem, hbm],
        scratch_shapes=[
            half, half, half, half,
            pltpu.VMEM((keys, HD), jnp.bfloat16),
            pltpu.VMEM((keys, 2 * HD), jnp.bfloat16),
            pltpu.VMEM((rows, KEY_CHUNK + suf), jnp.float32),
            pltpu.VMEM((prompts, units, rows, width), jnp.bfloat16),
            pltpu.VMEM((features, columns), jnp.bfloat16),
            pltpu.VMEM((prompts, rows, columns), jnp.float32),
            pltpu.VMEM((prompts, rows, col_count), jnp.bfloat16),
            pltpu.VMEM((prompts, rows, col_count), jnp.bfloat16),
            pltpu.VMEM((width, columns), jnp.bfloat16),
            pltpu.VMEM((rows, columns), jnp.float32),
            block, block, block, block,
            pltpu.VMEM((2, rows, keys), jnp.float32),
            dma((heads,)), dma((heads,)), dma((heads,)), dma((heads,)), dma((heads,)), dma((heads,)), dma((heads,)),
            dma((prompts, units)), dma((prompts, units)), dma((prompts, units)),
            dma((prompts,)), dma((prompts,)), dma,
            dma((units // 2,)), dma((units // 2,)), dma((units // 2,)), dma((units // 2,)), dma, dma, dma, dma, dma,
            dma((units,)),
        ],
        compiler_params=pltpu.CompilerParams(
            collective_id=0, has_side_effects=True, vmem_limit_bytes=62 * 1024 * 1024
        ),
        cost_estimate=pl.CostEstimate(
            flops=4 * rows * features * keys + 2 * prompts * rows * features * columns,
            bytes_accessed=4 * plen * heads * HD + 2 * features * columns,
            transcendentals=rows * (features // HD) * keys,
        ),
    )(
        owner_index, suffix_lengths.reshape(1), queries[0], suffix_kv[:, 0], prompt_cache[:, 0, 0], out_weight
    )[0]


def body(owner_index, suffix_lengths, queries, suffix_kv, prompt_cache, out_weight):
    cand_count = lax.axis_size("cand")
    prompt_count = lax.axis_size("prompt")
    tensor_count = lax.axis_size("tensor")
    if (cand_count, prompt_count, tensor_count) == (4, 4, 2):
        return fused(owner_index, suffix_lengths, queries, suffix_kv, prompt_cache, out_weight)
    owner = owner_index[0]
    me = lax.axis_index("cand")
    side = me % 2
    rows = queries.shape[1]
    kv_count = suffix_kv.shape[3] // HD
    group = queries.shape[2] // (kv_count * HD)

    cache = prompt_cache[:, 0, 0]
    keep = lax.dynamic_index_in_dim(cache, side, 0, keepdims=False)
    give = lax.dynamic_index_in_dim(cache, 1 - side, 0, keepdims=False)

    def same(bit):
        return (owner & bit) == (me & bit)

    pairs = []
    for head in range(kv_count):
        cols = slice(head * HD, (head + 1) * HD)
        got = lax.ppermute(give[:, cols], "cand", flip_perm(cand_count, 1))
        part = jnp.where(same(1), keep[:, cols], got)
        bit = 2
        while bit < cand_count:
            got = lax.ppermute(part, "cand", flip_perm(cand_count, bit))
            part = jnp.where(same(bit), part, got)
            bit *= 2
        pairs.append((part, lax.ppermute(part, "cand", flip_perm(cand_count, 1))))

    length = suffix_lengths.reshape(1)
    flip = side.reshape(1).astype(jnp.int32)
    query_rows = queries[0]
    gathered = []
    for head in range(kv_count):
        mine, other = pairs[head]
        done = attend_head(
            head, length, flip, query_rows, mine, other, suffix_kv[0, 0], suffix_kv[1, 0], group
        )
        gathered.append(lax.all_gather(done, "prompt", axis=0, tiled=True))

    def project(weight):
        total = None
        for head in range(kv_count):
            piece = weight[head * group * HD : (head + 1) * group * HD]
            part = jnp.dot(gathered[head], piece, preferred_element_type=jnp.float32)
            total = part if total is None else total + part
        return total

    col_count = out_weight.shape[1] // tensor_count
    if tensor_count == 2:
        here = lax.axis_index("tensor")
        theirs = lax.dynamic_slice_in_dim(out_weight, (1 - here) * col_count, col_count, 1)
        ours = lax.dynamic_slice_in_dim(out_weight, here * col_count, col_count, 1)
        sent = project(theirs).astype(jnp.bfloat16)
        arrived = lax.ppermute(sent, "tensor", flip_perm(2, 1))
        result = (project(ours) + arrived.astype(jnp.float32)).astype(jnp.bfloat16)
    else:
        total = project(out_weight)
        result = lax.psum_scatter(total, "tensor", scatter_dimension=1, tiled=True).astype(jnp.bfloat16)
    return result.reshape(prompt_count, rows, col_count)


def solution(mesh):
    in_specs = (
        P("prompt"),
        P("prompt", "cand"),
        P("prompt", "cand", "tensor"),
        P(None, "prompt", "cand", "tensor"),
        P(None, "prompt", "cand", None, "tensor"),
        P("tensor", "prompt"),
    )
    out_specs = P(None, "cand", ("prompt", "tensor"))
    return jax.shard_map(body, mesh=mesh, in_specs=in_specs, out_specs=out_specs, check_vma=False)
```
